32 devices in a mesh: leaf: 2 (over core), front: 16 (over z, y, x).
Axes of the slice: x: 2, y: 2, z: 4, core: 2. Of those that a mesh axis runs over, the one named last changes fastest.
Arguments:
- front_block: float32 [8192, 8192], P('leaf', 'front'), as said below
- child_update: float32 [2, 6144, 8192], P('leaf', None, 'front'), as said below
- child_map: int32 [2, 48], P('leaf'), may hold values from 0 to 63, as said below
Outputs:
- factored: float32 [8192, 8192], P('leaf', 'front')
The draws below stay inside these ranges and needn't reach their ends.
Inputs may be any that keep to these rules, and one draw needn't show every extreme that they name: `child_map`: each row is strictly increasing, holds 48 distinct blocks, and always names block 0 and block 63. `front_block`: Symmetric; the assembled front is positive definite. `child_update`: each child's update is symmetric and positive semidefinite in the child's order; columns of parent blocks that the child's map does not name are zero.
All inputs are finite; a program needn't handle non-finite values.
Results may differ from the reference program's by a relative error of at most 0.000088.
Values sent between devices are 32-bit elements; how exact they have to be, the bound alone decides.
No kernel may reach another device: no remote copies, remote signals or barrier semaphores. Data moves between devices by JAX's collectives and lax.ppermute only.
A program may use at most 128 MiB of HBM per device.

```python
import jax
import jax.numpy as jnp
from jax import lax

BLK = 128
PB = 64
CB = 48
P_SIZE = 8192
C = 6144
S = 512
NCH = 2


kernel_reach = 0.25


front_gain = 2.0


log_two = 0.6931471805599453


def distance_kernel(points):
    distance = jnp.abs(points[:, None, 0] - points[None, :, 0])
    distance = distance + jnp.abs(points[:, None, 1] - points[None, :, 1])
    distance = distance + jnp.abs(points[:, None, 2] - points[None, :, 2])
    return jnp.exp(-distance / kernel_reach)


def child_blocks(key):
    child_keys = jax.random.split(jax.random.fold_in(key, 7), NCH)

    def one_child(child_key):
        chosen = jax.random.permutation(child_key, PB - 2)[:CB - 2] + 1
        ends = jnp.array([0, PB - 1], dtype=jnp.int32)
        return jnp.sort(jnp.concatenate([ends, chosen.astype(jnp.int32)]))
    return jax.vmap(one_child)(child_keys)


def draw_child_map(key, part):
    return child_blocks(key).astype(jnp.int32)


def draw_child_update(key, part):
    blocks = child_blocks(key)
    offsets = jnp.arange(BLK, dtype=jnp.int32)

    def one_child(inputs):
        child, child_blocks_row = inputs
        child_key = jax.random.fold_in(jax.random.fold_in(key, 11), child)
        point_key = jax.random.fold_in(child_key, 0)
        points = jax.random.uniform(point_key, (C, 3), jnp.float32)
        symmetric = distance_kernel(points)
        col_index = (child_blocks_row[:, None] * BLK + offsets[None, :]).reshape(-1)
        return jnp.zeros((C, P_SIZE), jnp.float32).at[:, col_index].set(symmetric)
    return lax.map(one_child, (jnp.arange(NCH, dtype=jnp.int32), blocks))


def draw_front_block(key, part):
    point_key, diag_key = jax.random.split(jax.random.fold_in(key, 3), 2)
    points = jax.random.uniform(point_key, (P_SIZE, 3), jnp.float32)
    extra = jnp.exp(jax.random.uniform(diag_key, (P_SIZE,), jnp.float32, -log_two, log_two))
    return front_gain * distance_kernel(points) + jnp.diag(extra)


def setup_inputs(seed: int = 0) -> dict:
    splits = jax.random.split(jax.random.key(seed), 4)
    return {
        "front_block": draw_front_block(jax.random.fold_in(splits[3], 71), 0),
        "child_update": draw_child_update(jax.random.fold_in(splits[3], 71), 0),
        "child_map": draw_child_map(jax.random.fold_in(splits[3], 71), 0),
    }


def solve_right(factor, rows):
    return lax.linalg.triangular_solve(factor, rows, left_side=False, lower=True, transpose_a=True)

def reference(front_block, child_update, child_map):
    assembled = front_block
    offsets = jnp.arange(BLK, dtype=jnp.int32)
    for child in range(NCH):
        row_index = (child_map[child][:, None] * BLK + offsets[None, :]).reshape(-1).astype(jnp.int32)
        assembled = assembled.at[row_index].add(child_update[child])
    factor = jnp.linalg.cholesky(assembled[:S, :S])
    solved = solve_right(factor, assembled[:, :S])
    lower_rows = solved[S:]
    schur_part = assembled[S:, S:] - jnp.dot(lower_rows, lower_rows.T, precision=lax.Precision.HIGHEST)
    top_part = jnp.concatenate([factor, lower_rows.T], axis=1)
    bottom_part = jnp.concatenate([lower_rows, schur_part], axis=1)
    return jnp.concatenate([top_part, bottom_part], axis=0)
```

```python
import functools

import jax
import jax.numpy as jnp
from jax import lax
from jax.experimental import pallas as pl
from jax.experimental.pallas import tpu as pltpu
from jax.sharding import PartitionSpec as P

BLK = 128
S = 512
SUB = 8
ROWS = 512
MIB = 1024 * 1024


def lane_spread(tile, lane):
    return jnp.broadcast_to(tile[:, lane:lane + 1], tile.shape)


def row_spread(tile, row):
    return jnp.broadcast_to(tile[row:row + 1, :], tile.shape)


def eliminate_block(block):
    strips = BLK // SUB
    sub = lax.broadcasted_iota(jnp.int32, (SUB, BLK), 0)
    lane = lax.broadcasted_iota(jnp.int32, (SUB, BLK), 1)
    upper = [block[SUB * s:SUB * s + SUB, :] for s in range(strips)]
    lower = [jnp.where(lane == sub + SUB * s, 1.0, 0.0) for s in range(strips)]
    pivots = []
    for p in range(strips):
        first = SUB * p
        cols = [lane_spread(upper[p], first + j) for j in range(SUB)]
        a, x = upper[p], lower[p]
        recips = []
        pivot = jnp.zeros((SUB, BLK), jnp.float32)
        for j in range(SUB):
            d = row_spread(cols[j], j)
            recip = 1.0 / d
            recips.append(recip)
            pivot = jnp.where(sub == j, d, pivot)
            if j + 1 < SUB:
                m = jnp.where(sub > j, cols[j] * recip, 0.0)
                for k in range(j + 1, SUB):
                    cols[k] = cols[k] - m * row_spread(cols[k], j)
                a = a - m * row_spread(a, j)
                x = x - m * row_spread(x, j)
        upper[p], lower[p] = a, x
        pivots.append(pivot)
        if p + 1 == strips:
            break
        va = [row_spread(a, j) * recips[j] for j in range(SUB)]
        vx = [row_spread(x, j) * recips[j] for j in range(SUB)]
        for j in range(SUB - 2, -1, -1):
            for k in range(j + 1, SUB):
                c = row_spread(cols[k], j) * recips[j]
                va[j] = va[j] - c * va[k]
                vx[j] = vx[j] - c * vx[k]
        for s in range(p + 1, strips):
            b = [lane_spread(upper[s], first + j) for j in range(SUB)]
            upper[s] = upper[s] - (
                ((b[0] * va[0] + b[1] * va[1]) + (b[2] * va[2] + b[3] * va[3]))
                + ((b[4] * va[4] + b[5] * va[5]) + (b[6] * va[6] + b[7] * va[7]))
            )
            lower[s] = lower[s] - (
                ((b[0] * vx[0] + b[1] * vx[1]) + (b[2] * vx[2] + b[3] * vx[3]))
                + ((b[4] * vx[4] + b[5] * vx[5]) + (b[6] * vx[6] + b[7] * vx[7]))
            )
    return (
        jnp.concatenate(upper, axis=0),
        jnp.concatenate(lower, axis=0),
        jnp.concatenate(pivots, axis=0),
    )


def exact_dot(a, b, dims=((1,), (0,))):
    return lax.dot_general(
        a, b, (dims, ((), ())),
        precision=lax.Precision.HIGHEST,
        preferred_element_type=jnp.float32,
    )


def factor_kernel(place, diag_ref, cols_ref, top_ref, mult_ref, u_ref, x_ref):
    cc = cols_ref.shape[1]
    u_ref[...] = diag_ref[...]
    eye = lax.broadcasted_iota(jnp.int32, (S, S), 0) == lax.broadcasted_iota(
        jnp.int32, (S, S), 1)
    x_ref[...] = jnp.where(eye, 1.0, 0.0)

    @pl.loop(0, S // BLK)
    def _(step):
        start = pl.multiple_of(step * BLK, BLK)
        rows = pl.ds(start, BLK)
        block, inverse, pivots = eliminate_block(u_ref[rows, rows])
        scale = lax.rsqrt(pivots)
        scale = scale * (1.5 - 0.5 * pivots * scale * scale)
        r = lax.broadcasted_iota(jnp.int32, (BLK, BLK), 0)
        c = lax.broadcasted_iota(jnp.int32, (BLK, BLK), 1)
        block = jnp.where(c >= r, block * scale, 0.0)
        inverse = inverse * scale
        u = exact_dot(inverse, u_ref[rows, :])
        x = exact_dot(inverse, x_ref[rows, :])
        col = lax.broadcasted_iota(jnp.int32, (BLK, S), 1)
        u = jnp.where(col >= start + BLK, u, 0.0)

        @pl.when(step < S // BLK - 1)
        def _():
            u_ref[...] -= exact_dot(u, u, ((0,), (0,)))
            x_ref[...] -= exact_dot(u, x, ((0,), (0,)))

        u_ref[rows, :] = u
        u_ref[rows, rows] = block
        x_ref[rows, :] = x

    is_pivot = place[0] < S // cc
    start = pl.multiple_of(jnp.minimum(place[0], S // cc - 1) * cc, cc)
    solved = exact_dot(x_ref[...], cols_ref[...])
    top_ref[...] = jnp.where(is_pivot, u_ref[pl.ds(start, cc), :].T, solved)
    unit = lax.broadcasted_iota(jnp.int32, (S, cc), 0) == start + lax.broadcasted_iota(
        jnp.int32, (S, cc), 1)
    right = jnp.where(is_pivot, jnp.where(unit, -1.0, 0.0), solved)
    mult_ref[...] = exact_dot(x_ref[...], right, ((0,), (0,)))


def factor_and_solve(place, diag, cols):
    cc = cols.shape[1]
    vmem = pl.BlockSpec(memory_space=pltpu.VMEM)
    flops = 6 * (2 * S * S * cc * 2 + S * S * S * 2)
    return pl.pallas_call(
        factor_kernel,
        out_shape=[jax.ShapeDtypeStruct((S, cc), jnp.float32)] * 2,
        in_specs=[pl.BlockSpec(memory_space=pltpu.SMEM), vmem, vmem],
        out_specs=[vmem, vmem],
        scratch_shapes=[pltpu.VMEM((S, S), jnp.float32)] * 2,
        compiler_params=pltpu.CompilerParams(vmem_limit_bytes=32 * MIB),
        cost_estimate=pl.CostEstimate(
            flops=flops, bytes_accessed=4 * S * (S + 3 * cc), transcendentals=0),
        name="factor_and_solve",
    )(place, diag, cols)


def assemble_kernel(index, front_ref, own_ref, recv_ref, out_ref):
    step = pl.program_id(0)
    own = jnp.where(index[1, step] > 0, own_ref[...], 0.0)
    recv = jnp.where(index[3, step] > 0, recv_ref[...], 0.0)
    out_ref[...] = front_ref[...] + own + recv


def assemble(index, front, child, recv):
    rows, cc = front.shape
    spec = functools.partial(pl.BlockSpec, (BLK, cc))
    return pl.pallas_call(
        assemble_kernel,
        out_shape=jax.ShapeDtypeStruct((rows, cc), jnp.float32),
        grid_spec=pltpu.PrefetchScalarGridSpec(
            num_scalar_prefetch=1,
            grid=(rows // BLK,),
            in_specs=[
                spec(lambda i, index: (i, 0)),
                spec(lambda i, index: (index[0, i], 0)),
                spec(lambda i, index: (index[2, i], 0)),
            ],
            out_specs=spec(lambda i, index: (i, 0)),
        ),
        cost_estimate=pl.CostEstimate(
            flops=2 * rows * cc, bytes_accessed=16 * rows * cc, transcendentals=0),
        name="assemble",
    )(index, front, child, recv)


def finish_kernel(place, base_ref, panel_ref, mult_ref, top_ref, out_ref):
    cc = out_ref.shape[1]
    is_pivot = place[0] < S // cc
    is_top = jnp.logical_and(place[1] == 0, pl.program_id(0) * ROWS < S)

    @pl.when(is_top)
    def _():
        out_ref[...] = top_ref[...]

    @pl.when(jnp.logical_not(is_top))
    def _():
        product = lax.dot_general(
            panel_ref[...], mult_ref[...], (((1,), (0,)), ((), ())),
            precision=lax.Precision.HIGH,
            preferred_element_type=jnp.float32,
        )
        out_ref[...] = jnp.where(is_pivot, 0.0, base_ref[...]) - product


def finish(place, base, panel, mult, top):
    rows, cc = base.shape
    whole = pl.BlockSpec((S, cc), lambda i, place: (0, 0))
    return pl.pallas_call(
        finish_kernel,
        out_shape=jax.ShapeDtypeStruct((rows, cc), jnp.float32),
        grid_spec=pltpu.PrefetchScalarGridSpec(
            num_scalar_prefetch=1,
            grid=(rows // ROWS,),
            in_specs=[
                pl.BlockSpec((ROWS, cc), lambda i, place: (i, 0)),
                pl.BlockSpec((ROWS, S), lambda i, place: (i, 0)),
                whole,
                whole,
            ],
            out_specs=pl.BlockSpec((ROWS, cc), lambda i, place: (i, 0)),
        ),
        compiler_params=pltpu.CompilerParams(vmem_limit_bytes=32 * MIB),
        cost_estimate=pl.CostEstimate(
            flops=6 * rows * S * cc, bytes_accessed=4 * rows * (2 * cc + S),
            transcendentals=0),
        name="finish",
    )(place, base, panel, mult, top)


def block_places(blocks, first, count, shift, limit):
    parent = first + jnp.arange(count, dtype=jnp.int32)
    reached = jnp.sum((blocks[None, :] <= parent[:, None]).astype(jnp.int32), axis=1)
    there = jnp.sum((blocks[None, :] == parent[:, None]).astype(jnp.int32), axis=1)
    return jnp.clip(reached - 1 - shift, 0, limit - 1), there


def spread_pivot(cols, front_index, front_count, holders):
    leaf_index = lax.axis_index("leaf")
    half = S // 2
    mine = lax.dynamic_slice_in_dim(cols, leaf_index * half, half, 0)
    steps = []
    step = holders
    while step < front_count:
        steps.append(step)
        step *= 2
    pieces = []
    for order, part in ((steps, mine[:half // 2]), (steps[::-1], mine[half // 2:])):
        held = list(range(holders))
        part = jnp.where(front_index < holders, part, 0.0)
        for step in order:
            got = lax.ppermute(part, "front", [(f, f + step) for f in held])
            part = part + got
            held += [f + step for f in held]
        pieces.append(part)
    mine = jnp.concatenate(pieces, axis=0)
    if holders > 1:
        groups = [list(range(f, f + holders)) for f in range(0, front_count, holders)]
        mine = lax.all_gather(mine, "front", axis_index_groups=groups, axis=1, tiled=True)
    other = lax.ppermute(mine, "leaf", [(0, 1), (1, 0)])
    low = jnp.where(leaf_index == 0, mine, other)
    high = jnp.where(leaf_index == 0, other, mine)
    return jnp.concatenate([low, high], axis=0)


def per_device(front_block, child_update, child_map):
    row_count, col_count = front_block.shape
    front_count = lax.axis_size("front")
    leaf_index = lax.axis_index("leaf")
    front_index = lax.axis_index("front")
    place = jnp.stack([front_index, leaf_index]).astype(jnp.int32)
    swap = [(0, 1), (1, 0)]
    child = child_update[0]
    blocks = child_map[0]
    child_blocks = blocks.shape[0]
    parent_blocks = row_count // BLK

    placed = []
    for b in range(S // BLK):
        total = jnp.where(leaf_index == 0, front_block[b * BLK:(b + 1) * BLK], 0.0)
        for k in range(b + 1):
            total = total + jnp.where(blocks[k] == b, child[k * BLK:(k + 1) * BLK], 0.0)
        placed.append(total)
    placed = jnp.concatenate(placed, axis=0)
    cols = placed + lax.ppermute(placed, "leaf", swap)

    half = front_count // 2
    piece = cols.T
    pairs = [(f, f + half) for f in range(half)]
    pairs += [(front_count + f + half, front_count + f) for f in range(half)]
    came = lax.ppermute(piece, ("leaf", "front"), pairs)
    piece = jnp.where((front_index >= half) == (leaf_index == 1), piece, came)
    groups = [list(range(half)), list(range(half, front_count))]
    panel = lax.all_gather(piece, "front", axis_index_groups=groups, axis=0, tiled=True)

    diag = spread_pivot(cols, front_index, front_count, S // col_count)

    sent = lax.dynamic_slice_in_dim(
        child, (1 - leaf_index) * (child_blocks - parent_blocks) * BLK, row_count, 0)
    recv = lax.ppermute(sent, "leaf", swap)
    other_blocks = lax.ppermute(blocks, "leaf", swap)
    first = leaf_index * parent_blocks
    shift = leaf_index * (child_blocks - parent_blocks)
    index = jnp.stack(
        block_places(blocks, first, parent_blocks, 0, child_blocks)
        + block_places(other_blocks, first, parent_blocks, shift, parent_blocks))
    base = assemble(index, front_block, child, recv)

    top, mult = factor_and_solve(place, diag, cols)
    return finish(place, base, panel, mult, top)


def solution(mesh):
    return jax.shard_map(
        per_device,
        mesh=mesh,
        in_specs=(P("leaf", "front"), P("leaf", None, "front"), P("leaf", None)),
        out_specs=P("leaf", "front"),
        check_vma=False,
    )
```

```python
import functools

import jax
import jax.numpy as jnp
from jax import lax
from jax.experimental import pallas as pl
from jax.experimental.pallas import tpu as pltpu
from jax.sharding import PartitionSpec as P

BLK = 128
S = 512
SUB = 8
MIB = 1024 * 1024


def lane_spread(tile, lane):
    return jnp.broadcast_to(tile[:, lane:lane + 1], tile.shape)


def row_spread(tile, row):
    return jnp.broadcast_to(tile[row:row + 1, :], tile.shape)


def eliminate_block(block):
    strips = BLK // SUB
    sub = lax.broadcasted_iota(jnp.int32, (SUB, BLK), 0)
    lane = lax.broadcasted_iota(jnp.int32, (SUB, BLK), 1)
    upper = [block[SUB * s:SUB * s + SUB, :] for s in range(strips)]
    lower = [jnp.where(lane == sub + SUB * s, 1.0, 0.0) for s in range(strips)]
    pivots = []
    for p in range(strips):
        first = SUB * p
        cols = [lane_spread(upper[p], first + j) for j in range(SUB)]
        a, x = upper[p], lower[p]
        recips = []
        pivot = jnp.zeros((SUB, BLK), jnp.float32)
        for j in range(SUB):
            d = row_spread(cols[j], j)
            recip = 1.0 / d
            recips.append(recip)
            pivot = jnp.where(sub == j, d, pivot)
            if j + 1 < SUB:
                m = jnp.where(sub > j, cols[j] * recip, 0.0)
                for k in range(j + 1, SUB):
                    cols[k] = cols[k] - m * row_spread(cols[k], j)
                a = a - m * row_spread(a, j)
                x = x - m * row_spread(x, j)
        upper[p], lower[p] = a, x
        pivots.append(pivot)
        if p + 1 == strips:
            break
        va = [row_spread(a, j) * recips[j] for j in range(SUB)]
        vx = [row_spread(x, j) * recips[j] for j in range(SUB)]
        for j in range(SUB - 2, -1, -1):
            for k in range(j + 1, SUB):
                c = row_spread(cols[k], j) * recips[j]
                va[j] = va[j] - c * va[k]
                vx[j] = vx[j] - c * vx[k]
        for s in range(p + 1, strips):
            b = [lane_spread(upper[s], first + j) for j in range(SUB)]
            upper[s] = upper[s] - (
                ((b[0] * va[0] + b[1] * va[1]) + (b[2] * va[2] + b[3] * va[3]))
                + ((b[4] * va[4] + b[5] * va[5]) + (b[6] * va[6] + b[7] * va[7]))
            )
            lower[s] = lower[s] - (
                ((b[0] * vx[0] + b[1] * vx[1]) + (b[2] * vx[2] + b[3] * vx[3]))
                + ((b[4] * vx[4] + b[5] * vx[5]) + (b[6] * vx[6] + b[7] * vx[7]))
            )
    return (
        jnp.concatenate(upper, axis=0),
        jnp.concatenate(lower, axis=0),
        jnp.concatenate(pivots, axis=0),
    )


def exact_dot(a, b, dims=((1,), (0,))):
    return lax.dot_general(
        a, b, (dims, ((), ())),
        precision=lax.Precision.HIGHEST,
        preferred_element_type=jnp.float32,
    )


def vmem_specs(count):
    return [pl.BlockSpec(memory_space=pltpu.VMEM)] * count


def pivot_rows_kernel(place, blocks, front_ref, child_ref, out_ref):
    for b in range(S // BLK):
        rows = slice(b * BLK, (b + 1) * BLK)
        total = jnp.where(place[1] == 0, front_ref[rows, :], 0.0)
        for k in range(b + 1):
            total += jnp.where(blocks[k] == b, child_ref[k * BLK:(k + 1) * BLK, :], 0.0)
        out_ref[rows, :] = total


def pivot_rows(place, blocks, front, child):
    cc = front.shape[1]
    smem = pl.BlockSpec(memory_space=pltpu.SMEM)
    first = pl.BlockSpec((S, cc), lambda i: (0, 0))
    return pl.pallas_call(
        pivot_rows_kernel,
        out_shape=jax.ShapeDtypeStruct((S, cc), jnp.float32),
        grid=(1,),
        in_specs=[smem, smem, first, first],
        out_specs=first,
        compiler_params=pltpu.CompilerParams(vmem_limit_bytes=56 * MIB),
        cost_estimate=pl.CostEstimate(
            flops=4 * S * cc, bytes_accessed=12 * S * cc, transcendentals=0),
        name="pivot_rows",
    )(place, blocks, front, child)


def packed_blocks():
    count = S // BLK
    order = [(i, j) for i in range(count) for j in range(i, count)]
    return order[:len(order) // 2], order[len(order) // 2:]


def block_slices(block):
    i, j = block
    return slice(i * BLK, (i + 1) * BLK), slice(j * BLK, (j + 1) * BLK)


def pivot_sum_kernel(place, mine_ref, other_ref, cols_ref, piece_ref, *packed):
    cols = mine_ref[...] + other_ref[...]
    cols_ref[...] = cols
    piece_ref[...] = cols.T
    if packed:
        low, high = packed_blocks()
        size = packed[0].shape[0]
        for n, blocks in enumerate(zip(low, high)):
            a, b = (cols[block_slices(block)] for block in blocks)
            value = jnp.where(place[1] == 0, a, b)
            value = jnp.where(place[0] == 0, value, 0.0)
            for ref, start in zip(packed, (0, size)):
                begin = max(n * BLK, start)
                end = min((n + 1) * BLK, start + size)
                if begin < end:
                    ref[begin - start:end - start, :] = value[begin - n * BLK:end - n * BLK]


def pivot_sum(place, mine, other):
    cc = mine.shape[1]
    shapes = [(S, cc), (cc, S)]
    if cc == S:
        shapes += [(len(packed_blocks()[0]) * BLK // 2, BLK)] * 2
    return pl.pallas_call(
        pivot_sum_kernel,
        out_shape=[jax.ShapeDtypeStruct(shape, jnp.float32) for shape in shapes],
        in_specs=[pl.BlockSpec(memory_space=pltpu.SMEM)] + vmem_specs(2),
        out_specs=vmem_specs(len(shapes)),
        compiler_params=pltpu.CompilerParams(vmem_limit_bytes=16 * MIB),
        cost_estimate=pl.CostEstimate(
            flops=S * cc, bytes_accessed=16 * S * cc, transcendentals=0),
        name="pivot_sum",
    )(place, mine, other)


def factor_step(step, u_ref, x_ref):
    rows = slice(step * BLK, (step + 1) * BLK)
    done, rest = slice(0, (step + 1) * BLK), slice((step + 1) * BLK, S)
    block, inverse, pivots = eliminate_block(u_ref[rows, rows])
    scale = lax.rsqrt(pivots)
    scale = scale * (1.5 - 0.5 * pivots * scale * scale)
    r = lax.broadcasted_iota(jnp.int32, (BLK, BLK), 0)
    c = lax.broadcasted_iota(jnp.int32, (BLK, BLK), 1)
    u_ref[rows, rows] = jnp.where(c >= r, block * scale, 0.0)
    inverse = inverse * scale
    x = exact_dot(inverse, x_ref[rows, done])
    x_ref[rows, done] = x
    if step:
        u_ref[rows, :step * BLK] = jnp.zeros((BLK, step * BLK), jnp.float32)
    if step + 1 < S // BLK:
        u = exact_dot(inverse, u_ref[rows, rest])
        u_ref[rows, rest] = u
        u_ref[rest, rest] -= exact_dot(u, u, ((0,), (0,)))
        x_ref[rest, done] -= exact_dot(u, x, ((0,), (0,)))


def first_step_kernel(place, *refs):
    u_ref, x_ref = refs[-2:]
    sources = refs[:-2]
    if len(sources) == 1:
        u_ref[...] = sources[0][...]
    else:
        mine = jnp.concatenate([ref[...] for ref in sources[:2]], axis=0)
        other = jnp.concatenate([ref[...] for ref in sources[2:]], axis=0)
        values = [
            jnp.where(place[1] == 0, mine, other), jnp.where(place[1] == 0, other, mine)]
        for value, blocks in zip(values, packed_blocks()):
            for n, block in enumerate(blocks):
                u_ref[block_slices(block)] = value[n * BLK:(n + 1) * BLK]
    eye = lax.broadcasted_iota(jnp.int32, (S, S), 0) == lax.broadcasted_iota(
        jnp.int32, (S, S), 1)
    x_ref[...] = jnp.where(eye, 1.0, 0.0)
    factor_step(0, u_ref, x_ref)


def middle_step_kernel(step, u_in, x_in, u_ref, x_ref):
    u_ref[...] = u_in[...]
    x_ref[...] = x_in[...]
    factor_step(step, u_ref, x_ref)


def last_step_kernel(place, u_in, x_in, cols_ref, top_ref, mult_ref, u_ref, x_ref):
    u_ref[...] = u_in[...]
    x_ref[...] = x_in[...]
    factor_step(S // BLK - 1, u_ref, x_ref)
    cc = cols_ref.shape[1]
    is_pivot = place[0] < S // cc
    start = pl.multiple_of(jnp.minimum(place[0], S // cc - 1) * cc, cc)
    solved = exact_dot(x_ref[...], cols_ref[...])
    top_ref[...] = jnp.where(is_pivot, u_ref[pl.ds(start, cc), :].T, solved)
    unit = lax.broadcasted_iota(jnp.int32, (S, cc), 0) == start + lax.broadcasted_iota(
        jnp.int32, (S, cc), 1)
    right = jnp.where(is_pivot, jnp.where(unit, -1.0, 0.0), solved)
    mult_ref[...] = exact_dot(x_ref[...], right, ((0,), (0,)))


FACTOR_PARAMS = dict(
    compiler_params=pltpu.CompilerParams(vmem_limit_bytes=48 * MIB),
    cost_estimate=pl.CostEstimate(
        flops=10 ** 6, bytes_accessed=4 * S, transcendentals=0),
)
SQUARE = jax.ShapeDtypeStruct((S, S), jnp.float32)


def first_step(place, sources):
    return pl.pallas_call(
        first_step_kernel,
        out_shape=[SQUARE] * 2,
        in_specs=[pl.BlockSpec(memory_space=pltpu.SMEM)] + vmem_specs(len(sources)),
        out_specs=vmem_specs(2),
        name="factor_step",
        **FACTOR_PARAMS,
    )(place, *sources)


def middle_step(step, u, x):
    return pl.pallas_call(
        functools.partial(middle_step_kernel, step),
        out_shape=[SQUARE] * 2,
        in_specs=vmem_specs(2),
        out_specs=vmem_specs(2),
        name="factor_step",
        **FACTOR_PARAMS,
    )(u, x)


def last_step(place, u, x, cols):
    return pl.pallas_call(
        last_step_kernel,
        out_shape=[jax.ShapeDtypeStruct(cols.shape, jnp.float32)] * 2,
        in_specs=[pl.BlockSpec(memory_space=pltpu.SMEM)] + vmem_specs(3),
        out_specs=vmem_specs(2),
        scratch_shapes=[pltpu.VMEM((S, S), jnp.float32)] * 2,
        name="factor_and_solve",
        **FACTOR_PARAMS,
    )(place, u, x, cols)


def finish_kernel(slots, place, index, front_ref, *refs):
    sub = front_ref.shape[0] // BLK
    own, recv, refs = refs[:sub], refs[sub:2 * sub], refs[2 * sub:]
    pieces, refs = refs[:len(slots)], refs[len(slots):]
    mult_ref, top_ref, out_ref = refs[0], refs[1], refs[-1]
    step = pl.program_id(0)
    cc = out_ref.shape[1]
    is_pivot = place[0] < S // cc
    for n, slot in enumerate(slots):
        block = jnp.bitwise_xor(place[2], slot)
        is_top = jnp.logical_and(place[1] == 0, block < S // cc)

        @pl.when(jnp.logical_and(step == n, is_top))
        def _():
            out_ref[...] = top_ref[pl.ds(pl.multiple_of(block * cc, cc), cc), :]

        @pl.when(jnp.logical_and(step == n, jnp.logical_not(is_top)))
        def _():
            product = lax.dot_general(
                pieces[n][...], mult_ref[...], (((1,), (0,)), ((), ())),
                precision=lax.Precision.HIGH,
                preferred_element_type=jnp.float32,
            )
            for j in range(sub):
                rows = slice(j * BLK, (j + 1) * BLK)
                at = block * sub + j
                base = front_ref[rows, :]
                base += jnp.where(index[1, at] > 0, own[j][...], 0.0)
                base += jnp.where(index[3, at] > 0, recv[j][...], 0.0)
                out_ref[rows, :] = jnp.where(is_pivot, 0.0, base) - product[rows, :]


def finish(place, index, front, child, recv, slots, pieces, mult, top, out=None):
    rows, cc = front.shape
    sub = cc // BLK

    def block_of(i, place):
        slot = jnp.int32(slots[0])
        for n in range(1, len(slots)):
            slot = jnp.where(i == n, slots[n], slot)
        return jnp.bitwise_xor(place[2], slot)

    def whole(shape):
        return pl.BlockSpec(shape, lambda i, place, index: (0, 0))

    def picked(row, j):
        return pl.BlockSpec(
            (BLK, cc), lambda i, place, index: (index[row, block_of(i, place) * sub + j], 0))

    moving = pl.BlockSpec((cc, cc), lambda i, place, index: (block_of(i, place), 0))
    count = len(slots)
    operands = [front] + [child] * sub + [recv] * sub + list(pieces) + [mult, top]
    specs = [moving] + [picked(0, j) for j in range(sub)] + [picked(2, j) for j in range(sub)]
    specs += [whole((cc, S))] * count + [whole((S, cc))] * 2
    aliases = {}
    if out is not None:
        aliases = {2 + len(operands): 0}
        operands.append(out)
        specs.append(pl.BlockSpec(memory_space=pl.ANY))
    return pl.pallas_call(
        functools.partial(finish_kernel, tuple(slots)),
        out_shape=jax.ShapeDtypeStruct((rows, cc), jnp.float32),
        grid_spec=pltpu.PrefetchScalarGridSpec(
            num_scalar_prefetch=2,
            grid=(count,),
            in_specs=specs,
            out_specs=moving,
        ),
        input_output_aliases=aliases,
        compiler_params=pltpu.CompilerParams(vmem_limit_bytes=48 * MIB),
        cost_estimate=pl.CostEstimate(
            flops=6 * count * cc * S * cc, bytes_accessed=4 * count * cc * (4 * cc + S),
            transcendentals=0),
        name="finish",
    )(place, index, *operands)


def block_places(blocks, first, count, shift, limit):
    parent = first + jnp.arange(count, dtype=jnp.int32)
    reached = jnp.sum((blocks[None, :] <= parent[:, None]).astype(jnp.int32), axis=1)
    there = jnp.sum((blocks[None, :] == parent[:, None]).astype(jnp.int32), axis=1)
    return jnp.clip(reached - 1 - shift, 0, limit - 1), there


def spread_pivot(cols, front_index, front_count, holders):
    leaf_index = lax.axis_index("leaf")
    half = S // 2
    mine = lax.dynamic_slice_in_dim(cols, leaf_index * half, half, 0)
    steps = []
    step = holders
    while step < front_count:
        steps.append(step)
        step *= 2
    pieces = []
    for order, part in ((steps, mine[:half // 2]), (steps[::-1], mine[half // 2:])):
        held = list(range(holders))
        part = jnp.where(front_index < holders, part, 0.0)
        for step in order:
            got = lax.ppermute(part, "front", [(f, f + step) for f in held])
            part = part + got
            held += [f + step for f in held]
        pieces.append(part)
    mine = jnp.concatenate(pieces, axis=0)
    if holders > 1:
        groups = [list(range(f, f + holders)) for f in range(0, front_count, holders)]
        mine = lax.all_gather(mine, "front", axis_index_groups=groups, axis=1, tiled=True)
    other = lax.ppermute(mine, "leaf", [(0, 1), (1, 0)])
    low = jnp.where(leaf_index == 0, mine, other)
    high = jnp.where(leaf_index == 0, other, mine)
    return jnp.concatenate([low, high], axis=0)


def spread_packed(parts, front_count, begin, middle, others):
    steps = [1 << n for n in range(front_count.bit_length() - 1)]
    orders = (steps, [steps[1], steps[0]] + steps[2:][::-1])
    helds = ([0], [0])
    for n in range(len(steps)):
        got = []
        for order, held, part in zip(orders, helds, parts):
            step = order[n]
            got.append(part + lax.ppermute(part, "front", [(f, f + step) for f in held]))
            held.extend([f + step for f in held])
        parts = got
        if n == 0:
            parts, begin = lax.optimization_barrier((parts, begin))
            work = middle(begin)
        elif n == 1:
            parts, work, others = lax.optimization_barrier((parts, work, others))
    return parts, work, others


def per_device(front_block, child_update, child_map):
    row_count, col_count = front_block.shape
    front_count = lax.axis_size("front")
    leaf_index = lax.axis_index("leaf")
    front_index = lax.axis_index("front")
    half = front_count // 2
    place = jnp.stack([front_index, leaf_index, front_index % half]).astype(jnp.int32)
    swap = [(0, 1), (1, 0)]
    child = child_update[0]
    blocks = child_map[0]
    child_blocks = blocks.shape[0]
    parent_blocks = row_count // BLK

    mine = pivot_rows(place, blocks, front_block, child)
    cols, piece, *packed = pivot_sum(place, mine, lax.ppermute(mine, "leaf", swap))

    pairs = [(f, f + half) for f in range(half)]
    pairs += [(front_count + f + half, front_count + f) for f in range(half)]
    came = lax.ppermute(piece, ("leaf", "front"), pairs)

    other_blocks = lax.ppermute(blocks, "leaf", swap)
    first = leaf_index * parent_blocks
    shift = leaf_index * (child_blocks - parent_blocks)
    index = jnp.stack(
        block_places(blocks, first, parent_blocks, 0, child_blocks)
        + block_places(other_blocks, first, parent_blocks, shift, parent_blocks))

    def rows_to_send(leaf):
        return lax.dynamic_slice_in_dim(
            child, (1 - leaf) * (child_blocks - parent_blocks) * BLK, row_count, 0)

    if packed:
        sources, sent, (came, index) = spread_packed(
            packed, front_count, leaf_index, rows_to_send, (came, index))
        sources = sources + [lax.ppermute(part, "leaf", swap) for part in sources]
    else:
        sources = [spread_pivot(cols, front_index, front_count, S // col_count)]
        sent = rows_to_send(leaf_index)
    piece = jnp.where((front_index >= half) == (leaf_index == 1), piece, came)

    def across(value, bit):
        flat = [(f, f ^ bit) for f in range(front_count)]
        return lax.ppermute(value, "front", flat)

    held = {0: piece}
    bit = half // 2
    sides = {}
    while bit > 2:
        for slot in list(held):
            if slot == 0:
                sides[1], sides[2] = across(held[0], 1), across(held[0], 2)
            held[slot + bit] = across(held[slot], bit)
        bit //= 2
    early = list(held)[:len(held) // 2]

    sources, held, sides = lax.optimization_barrier((sources, held, sides))
    for slot in held:
        if slot:
            sides[slot + 1], sides[slot + 2] = across(held[slot], 1), across(held[slot], 2)
    u, x = first_step(place, sources)
    u, x = middle_step(1, u, x)
    u, x, sides = lax.optimization_barrier((u, x, sides))
    crossed = {}
    for slot in held:
        if slot in early:
            crossed[slot + 3] = across(sides[slot + 1], 2)
        else:
            crossed[slot + 3] = across(sides[slot + 2], 1)
    u, x = middle_step(2, u, x)
    u, x, sent = lax.optimization_barrier((u, x, sent))
    recv = lax.ppermute(sent, "leaf", swap)
    top, mult = last_step(place, u, x, cols)

    held.update(sides)
    out = None
    for group in (held, crossed):
        out = finish(
            place, index, front_block, child, recv, list(group), list(group.values()),
            mult, top, out)
    return out


def solution(mesh):
    return jax.shard_map(
        per_device,
        mesh=mesh,
        in_specs=(P("leaf", "front"), P("leaf", None, "front"), P("leaf", None)),
        out_specs=P("leaf", "front"),
        check_vma=False,
    )
```

```python
import functools

import jax
import jax.numpy as jnp
from jax import lax
from jax.experimental import pallas as pl
from jax.experimental.pallas import tpu as pltpu
from jax.sharding import PartitionSpec as P

BLK = 128
S = 512
SUB = 8
MIB = 1024 * 1024


def lane_spread(tile, lane):
    return jnp.broadcast_to(tile[:, lane:lane + 1], tile.shape)


def row_spread(tile, row):
    return jnp.broadcast_to(tile[row:row + 1, :], tile.shape)


def eliminate_block(block):
    strips = BLK // SUB
    sub = lax.broadcasted_iota(jnp.int32, (SUB, BLK), 0)
    lane = lax.broadcasted_iota(jnp.int32, (SUB, BLK), 1)
    upper = [block[SUB * s:SUB * s + SUB, :] for s in range(strips)]
    lower = [jnp.where(lane == sub + SUB * s, 1.0, 0.0) for s in range(strips)]
    pivots = []
    for p in range(strips):
        first = SUB * p
        cols = [lane_spread(upper[p], first + j) for j in range(SUB)]
        a, x = upper[p], lower[p]
        recips = []
        pivot = jnp.zeros((SUB, BLK), jnp.float32)
        for j in range(SUB):
            d = row_spread(cols[j], j)
            recip = 1.0 / d
            recips.append(recip)
            pivot = jnp.where(sub == j, d, pivot)
            if j + 1 < SUB:
                m = jnp.where(sub > j, cols[j] * recip, 0.0)
                for k in range(j + 1, SUB):
                    cols[k] = cols[k] - m * row_spread(cols[k], j)
                a = a - m * row_spread(a, j)
                x = x - m * row_spread(x, j)
        upper[p], lower[p] = a, x
        pivots.append(pivot)
        if p + 1 == strips:
            break
        va = [row_spread(a, j) * recips[j] for j in range(SUB)]
        vx = [row_spread(x, j) * recips[j] for j in range(SUB)]
        for j in range(SUB - 2, -1, -1):
            for k in range(j + 1, SUB):
                c = row_spread(cols[k], j) * recips[j]
                va[j] = va[j] - c * va[k]
                vx[j] = vx[j] - c * vx[k]
        for s in range(p + 1, strips):
            b = [lane_spread(upper[s], first + j) for j in range(SUB)]
            upper[s] = upper[s] - (
                ((b[0] * va[0] + b[1] * va[1]) + (b[2] * va[2] + b[3] * va[3]))
                + ((b[4] * va[4] + b[5] * va[5]) + (b[6] * va[6] + b[7] * va[7]))
            )
            lower[s] = lower[s] - (
                ((b[0] * vx[0] + b[1] * vx[1]) + (b[2] * vx[2] + b[3] * vx[3]))
                + ((b[4] * vx[4] + b[5] * vx[5]) + (b[6] * vx[6] + b[7] * vx[7]))
            )
    return (
        jnp.concatenate(upper, axis=0),
        jnp.concatenate(lower, axis=0),
        jnp.concatenate(pivots, axis=0),
    )


def exact_dot(a, b, dims=((1,), (0,))):
    return lax.dot_general(
        a, b, (dims, ((), ())),
        precision=lax.Precision.HIGHEST,
        preferred_element_type=jnp.float32,
    )


def vmem_specs(count):
    return [pl.BlockSpec(memory_space=pltpu.VMEM)] * count


def pivot_rows_kernel(place, blocks, front_hbm, child_hbm, out_ref, front_ref, child_ref, sems):
    front = pltpu.make_async_copy(front_hbm.at[:S, :], front_ref, sems.at[0])
    child = pltpu.make_async_copy(child_hbm.at[:S, :], child_ref, sems.at[1])
    front.start()
    child.start()
    front.wait()
    child.wait()
    for b in range(S // BLK):
        rows = slice(b * BLK, (b + 1) * BLK)
        total = jnp.where(place[1] == 0, front_ref[rows, :], 0.0)
        for k in range(b + 1):
            total += jnp.where(blocks[k] == b, child_ref[k * BLK:(k + 1) * BLK, :], 0.0)
        out_ref[rows, :] = total


def pivot_rows(place, blocks, front, child):
    cc = front.shape[1]
    smem = pl.BlockSpec(memory_space=pltpu.SMEM)
    hbm = pl.BlockSpec(memory_space=pl.ANY)
    return pl.pallas_call(
        pivot_rows_kernel,
        out_shape=jax.ShapeDtypeStruct((S, cc), jnp.float32),
        in_specs=[smem, smem, hbm, hbm],
        out_specs=pl.BlockSpec(memory_space=pltpu.VMEM),
        scratch_shapes=[pltpu.VMEM((S, cc), jnp.float32)] * 2
        + [pltpu.SemaphoreType.DMA((2,))],
        compiler_params=pltpu.CompilerParams(vmem_limit_bytes=56 * MIB),
        cost_estimate=pl.CostEstimate(
            flops=4 * S * cc, bytes_accessed=12 * S * cc, transcendentals=0),
        name="pivot_rows",
    )(place, blocks, front, child)


def packed_blocks():
    count = S // BLK
    order = [(i, j) for i in range(count) for j in range(i, count)]
    return order[:len(order) // 2], order[len(order) // 2:]


def block_slices(block):
    i, j = block
    return slice(i * BLK, (i + 1) * BLK), slice(j * BLK, (j + 1) * BLK)


def pivot_sum_kernel(place, mine_ref, other_ref, cols_ref, piece_ref, *packed):
    cols = mine_ref[...] + other_ref[...]
    cols_ref[...] = cols
    piece_ref[...] = cols.T
    if packed:
        for n, blocks in enumerate(zip(*packed_blocks())):
            low, high = (cols[block_slices(block)] for block in blocks)
            value = jnp.where(place[1] == 0, low, high)
            packed[0][n * BLK:(n + 1) * BLK, :] = jnp.where(place[0] == 0, value, 0.0)


def pivot_sum(place, mine, other):
    cc = mine.shape[1]
    shapes = [(S, cc), (cc, S)]
    if cc == S:
        shapes.append((len(packed_blocks()[0]) * BLK, BLK))
    return pl.pallas_call(
        pivot_sum_kernel,
        out_shape=[jax.ShapeDtypeStruct(shape, jnp.float32) for shape in shapes],
        in_specs=[pl.BlockSpec(memory_space=pltpu.SMEM)] + vmem_specs(2),
        out_specs=vmem_specs(len(shapes)),
        compiler_params=pltpu.CompilerParams(vmem_limit_bytes=16 * MIB),
        cost_estimate=pl.CostEstimate(
            flops=S * cc, bytes_accessed=16 * S * cc, transcendentals=0),
        name="pivot_sum",
    )(place, mine, other)


def factor_step(step, u_ref, x_ref):
    rows = slice(step * BLK, (step + 1) * BLK)
    done, rest = slice(0, (step + 1) * BLK), slice((step + 1) * BLK, S)
    block, inverse, pivots = eliminate_block(u_ref[rows, rows])
    scale = lax.rsqrt(pivots)
    scale = scale * (1.5 - 0.5 * pivots * scale * scale)
    r = lax.broadcasted_iota(jnp.int32, (BLK, BLK), 0)
    c = lax.broadcasted_iota(jnp.int32, (BLK, BLK), 1)
    u_ref[rows, rows] = jnp.where(c >= r, block * scale, 0.0)
    inverse = inverse * scale
    x = exact_dot(inverse, x_ref[rows, done])
    x_ref[rows, done] = x
    if step:
        u_ref[rows, :step * BLK] = jnp.zeros((BLK, step * BLK), jnp.float32)
    if step + 1 < S // BLK:
        u = exact_dot(inverse, u_ref[rows, rest])
        u_ref[rows, rest] = u
        u_ref[rest, rest] -= exact_dot(u, u, ((0,), (0,)))
        x_ref[rest, done] -= exact_dot(u, x, ((0,), (0,)))


def first_step_kernel(place, *refs):
    u_ref, x_ref = refs[-2:]
    sources = refs[:-2]
    if len(sources) == 1:
        u_ref[...] = sources[0][...]
    else:
        mine = jnp.concatenate([ref[...] for ref in sources[:2]], axis=0)
        other = jnp.concatenate([ref[...] for ref in sources[2:]], axis=0)
        values = [
            jnp.where(place[1] == 0, mine, other), jnp.where(place[1] == 0, other, mine)]
        for value, blocks in zip(values, packed_blocks()):
            for n, block in enumerate(blocks):
                u_ref[block_slices(block)] = value[n * BLK:(n + 1) * BLK]
    eye = lax.broadcasted_iota(jnp.int32, (S, S), 0) == lax.broadcasted_iota(
        jnp.int32, (S, S), 1)
    x_ref[...] = jnp.where(eye, 1.0, 0.0)
    factor_step(0, u_ref, x_ref)


def middle_step_kernel(step, u_in, x_in, u_ref, x_ref):
    u_ref[...] = u_in[...]
    x_ref[...] = x_in[...]
    factor_step(step, u_ref, x_ref)


def last_step_kernel(place, u_in, x_in, cols_ref, top_ref, mult_ref, u_ref, x_ref):
    u_ref[...] = u_in[...]
    x_ref[...] = x_in[...]
    factor_step(S // BLK - 1, u_ref, x_ref)
    cc = cols_ref.shape[1]
    is_pivot = place[0] < S // cc
    start = pl.multiple_of(jnp.minimum(place[0], S // cc - 1) * cc, cc)
    solved = exact_dot(x_ref[...], cols_ref[...])
    top_ref[...] = jnp.where(is_pivot, u_ref[pl.ds(start, cc), :].T, solved)
    unit = lax.broadcasted_iota(jnp.int32, (S, cc), 0) == start + lax.broadcasted_iota(
        jnp.int32, (S, cc), 1)
    right = jnp.where(is_pivot, jnp.where(unit, -1.0, 0.0), solved)
    mult_ref[...] = exact_dot(x_ref[...], right, ((0,), (0,)))


FACTOR_PARAMS = dict(
    compiler_params=pltpu.CompilerParams(vmem_limit_bytes=48 * MIB),
    cost_estimate=pl.CostEstimate(
        flops=10 ** 6, bytes_accessed=4 * S, transcendentals=0),
)
SQUARE = jax.ShapeDtypeStruct((S, S), jnp.float32)


def first_step(place, sources):
    return pl.pallas_call(
        first_step_kernel,
        out_shape=[SQUARE] * 2,
        in_specs=[pl.BlockSpec(memory_space=pltpu.SMEM)] + vmem_specs(len(sources)),
        out_specs=vmem_specs(2),
        name="factor_step",
        **FACTOR_PARAMS,
    )(place, *sources)


def middle_step(step, u, x):
    return pl.pallas_call(
        functools.partial(middle_step_kernel, step),
        out_shape=[SQUARE] * 2,
        in_specs=vmem_specs(2),
        out_specs=vmem_specs(2),
        name="factor_step",
        **FACTOR_PARAMS,
    )(u, x)


def last_step(place, u, x, cols):
    return pl.pallas_call(
        last_step_kernel,
        out_shape=[jax.ShapeDtypeStruct(cols.shape, jnp.float32)] * 2,
        in_specs=[pl.BlockSpec(memory_space=pltpu.SMEM)] + vmem_specs(3),
        out_specs=vmem_specs(2),
        scratch_shapes=[pltpu.VMEM((S, S), jnp.float32)] * 2,
        name="factor_and_solve",
        **FACTOR_PARAMS,
    )(place, u, x, cols)


GROUP = 4


def assemble_kernel(index, front_ref, *refs):
    out_ref = refs[-1]
    step = pl.program_id(0)
    for j in range(GROUP):
        rows = slice(j * BLK, (j + 1) * BLK)
        block = step * GROUP + j
        own = jnp.where(index[1, block] > 0, refs[j][...], 0.0)
        recv = jnp.where(index[3, block] > 0, refs[GROUP + j][...], 0.0)
        out_ref[rows, :] = front_ref[rows, :] + own + recv


def assemble(index, front, child, recv):
    rows, cc = front.shape

    def picked(row, j):
        return pl.BlockSpec((BLK, cc), lambda i, index: (index[row, i * GROUP + j], 0))

    plain = pl.BlockSpec((GROUP * BLK, cc), lambda i, index: (i, 0))
    return pl.pallas_call(
        assemble_kernel,
        out_shape=jax.ShapeDtypeStruct((rows, cc), jnp.float32),
        grid_spec=pltpu.PrefetchScalarGridSpec(
            num_scalar_prefetch=1,
            grid=(rows // (GROUP * BLK),),
            in_specs=[plain]
            + [picked(0, j) for j in range(GROUP)]
            + [picked(2, j) for j in range(GROUP)],
            out_specs=plain,
        ),
        compiler_params=pltpu.CompilerParams(vmem_limit_bytes=44 * MIB),
        cost_estimate=pl.CostEstimate(
            flops=2 * rows * cc, bytes_accessed=16 * rows * cc, transcendentals=0),
        name="assemble",
    )(index, front, *[child] * GROUP, *[recv] * GROUP)


def finish_kernel(slots, place, base_hbm, mult_ref, top_ref, *refs):
    pieces, refs = refs[:len(slots)], refs[len(slots):]
    out_hbm, rows_ref, piece_ref, in_sems, piece_sems, out_sems = refs
    cc = mult_ref.shape[1]
    is_pivot = place[0] < S // cc
    blocks = [jnp.bitwise_xor(place[2], slot) for slot in slots]

    def rows_of(n):
        return pl.ds(pl.multiple_of(blocks[n] * cc, cc), cc)

    def base_copy(n):
        return pltpu.make_async_copy(base_hbm.at[rows_of(n), :], rows_ref.at[n], in_sems.at[n])

    def piece_copy(n):
        return pltpu.make_async_copy(pieces[n], piece_ref.at[n], piece_sems.at[n])

    def out_copy(n):
        return pltpu.make_async_copy(rows_ref.at[n], out_hbm.at[rows_of(n), :], out_sems.at[n])

    for n in range(len(slots)):
        piece_copy(n).start()
        base_copy(n).start()
    for n in range(len(slots)):
        piece_copy(n).wait()
        base_copy(n).wait()
        is_top = jnp.logical_and(place[1] == 0, blocks[n] < S // cc)

        @pl.when(is_top)
        def _():
            rows_ref[n] = top_ref[rows_of(n), :]

        @pl.when(jnp.logical_not(is_top))
        def _():
            product = lax.dot_general(
                piece_ref[n], mult_ref[...], (((1,), (0,)), ((), ())),
                precision=lax.Precision.HIGH,
                preferred_element_type=jnp.float32,
            )
            rows_ref[n] = jnp.where(is_pivot, 0.0, rows_ref[n]) - product

        out_copy(n).start()
    for n in range(len(slots)):
        out_copy(n).wait()


def finish(place, base, slots, pieces, mult, top):
    rows, cc = base.shape
    count = len(slots)
    hbm = pl.BlockSpec(memory_space=pl.ANY)
    return pl.pallas_call(
        functools.partial(finish_kernel, tuple(slots)),
        out_shape=jax.ShapeDtypeStruct((rows, cc), jnp.float32),
        in_specs=[pl.BlockSpec(memory_space=pltpu.SMEM), hbm] + vmem_specs(2) + [hbm] * count,
        out_specs=hbm,
        scratch_shapes=[
            pltpu.VMEM((count, cc, cc), jnp.float32),
            pltpu.VMEM((count, cc, S), jnp.float32),
        ]
        + [pltpu.SemaphoreType.DMA((count,))] * 3,
        input_output_aliases={1: 0},
        compiler_params=pltpu.CompilerParams(vmem_limit_bytes=48 * MIB),
        cost_estimate=pl.CostEstimate(
            flops=6 * count * cc * S * cc, bytes_accessed=4 * count * cc * (2 * cc + S),
            transcendentals=0),
        name="finish",
    )(place, base, mult, top, *pieces)


def block_places(blocks, first, count, shift, limit):
    parent = first + jnp.arange(count, dtype=jnp.int32)
    reached = jnp.sum((blocks[None, :] <= parent[:, None]).astype(jnp.int32), axis=1)
    there = jnp.sum((blocks[None, :] == parent[:, None]).astype(jnp.int32), axis=1)
    return jnp.clip(reached - 1 - shift, 0, limit - 1), there


def spread_pivot(cols, front_index, front_count, holders):
    leaf_index = lax.axis_index("leaf")
    half = S // 2
    mine = lax.dynamic_slice_in_dim(cols, leaf_index * half, half, 0)
    steps = []
    step = holders
    while step < front_count:
        steps.append(step)
        step *= 2
    pieces = []
    for order, part in ((steps, mine[:half // 2]), (steps[::-1], mine[half // 2:])):
        held = list(range(holders))
        part = jnp.where(front_index < holders, part, 0.0)
        for step in order:
            got = lax.ppermute(part, "front", [(f, f + step) for f in held])
            part = part + got
            held += [f + step for f in held]
        pieces.append(part)
    mine = jnp.concatenate(pieces, axis=0)
    if holders > 1:
        groups = [list(range(f, f + holders)) for f in range(0, front_count, holders)]
        mine = lax.all_gather(mine, "front", axis_index_groups=groups, axis=1, tiled=True)
    other = lax.ppermute(mine, "leaf", [(0, 1), (1, 0)])
    low = jnp.where(leaf_index == 0, mine, other)
    high = jnp.where(leaf_index == 0, other, mine)
    return jnp.concatenate([low, high], axis=0)


def pass_on(part, steps, n):
    held = [0]
    for step in steps[:n]:
        held += [f + step for f in held]
    return part + lax.ppermute(part, "front", [(f, f + steps[n]) for f in held])


def per_device(front_block, child_update, child_map):
    row_count, col_count = front_block.shape
    front_count = lax.axis_size("front")
    leaf_index = lax.axis_index("leaf")
    front_index = lax.axis_index("front")
    half = front_count // 2
    place = jnp.stack([front_index, leaf_index, front_index % half]).astype(jnp.int32)
    swap = [(0, 1), (1, 0)]
    child = child_update[0]
    blocks = child_map[0]
    child_blocks = blocks.shape[0]
    parent_blocks = row_count // BLK

    mine = pivot_rows(place, blocks, front_block, child)
    cols, piece, *packed = pivot_sum(place, mine, lax.ppermute(mine, "leaf", swap))

    pairs = [(f, f + half) for f in range(half)]
    pairs += [(front_count + f + half, front_count + f) for f in range(half)]
    came = lax.ppermute(piece, ("leaf", "front"), pairs)

    other_blocks = lax.ppermute(blocks, "leaf", swap)
    first = leaf_index * parent_blocks
    shift = leaf_index * (child_blocks - parent_blocks)
    index = jnp.stack(
        block_places(blocks, first, parent_blocks, 0, child_blocks)
        + block_places(other_blocks, first, parent_blocks, shift, parent_blocks))

    def rows_to_send(leaf):
        return lax.dynamic_slice_in_dim(
            child, (1 - leaf) * (child_blocks - parent_blocks) * BLK, row_count, 0)

    def across(value, bit):
        return lax.ppermute(value, "front", [(f, f ^ bit) for f in range(front_count)])

    if packed:
        passed, = packed
        steps, step = [], half
        while step > 2:
            steps.append(step)
            step //= 2
        passed = pass_on(passed, steps, 0)
        passed, later = lax.optimization_barrier((passed, leaf_index))
        sent = rows_to_send(later)
        for n in range(1, len(steps)):
            passed = pass_on(passed, steps, n)
        passed, sent, index, came = lax.optimization_barrier((passed, sent, index, came))
        recv = lax.ppermute(sent, "leaf", swap)
        middle = passed.shape[0] // 2
        parts = [passed[:middle], passed[middle:]]
        orders = [steps + [1, 2], steps + [2, 1]]
        for n in range(len(steps), len(steps) + 2):
            parts = [pass_on(part, order, n) for part, order in zip(parts, orders)]
            parts = lax.optimization_barrier(parts)
        parts, came = lax.optimization_barrier((parts, came))
        sources = parts + [lax.ppermute(part, "leaf", swap) for part in parts]
    else:
        recv = lax.ppermute(rows_to_send(leaf_index), "leaf", swap)
        sources = [spread_pivot(cols, front_index, front_count, S // col_count)]
    piece = jnp.where((front_index >= half) == (leaf_index == 1), piece, came)

    held, sides, crossed = {0: piece}, {}, {}
    sides[1], sides[2] = across(piece, 1), across(piece, 2)
    bit = half // 2
    while bit > 2:
        for slot in list(held):
            held[slot + bit] = across(held[slot], bit)
        bit //= 2
    early = list(held)[:len(held) // 2]

    out = assemble(index, front_block, child, recv)
    sources, out = lax.optimization_barrier((sources, out))
    u, x = first_step(place, sources)
    u, x, held, sides = lax.optimization_barrier((u, x, held, sides))
    for slot in held:
        if slot:
            sides[slot + 1], sides[slot + 2] = across(held[slot], 1), across(held[slot], 2)
    u, x = middle_step(1, u, x)
    u, x = middle_step(2, u, x)
    u, x, sides = lax.optimization_barrier((u, x, sides))
    for slot in held:
        if slot in early:
            crossed[slot + 3] = across(sides[slot + 1], 2)
        else:
            crossed[slot + 3] = across(sides[slot + 2], 1)
    top, mult = last_step(place, u, x, cols)

    held.update(sides)
    for group in (held, crossed):
        out = finish(place, out, list(group), list(group.values()), mult, top)
    return out


def solution(mesh):
    return jax.shard_map(
        per_device,
        mesh=mesh,
        in_specs=(P("leaf", "front"), P("leaf", None, "front"), P("leaf", None)),
        out_specs=P("leaf", "front"),
        check_vma=False,
    )
```

```python
import functools

import jax
import jax.numpy as jnp
from jax import lax
from jax.experimental import pallas as pl
from jax.experimental.pallas import tpu as pltpu
from jax.sharding import PartitionSpec as P

BLK = 128
S = 512
SUB = 8
MIB = 1024 * 1024


def lane_spread(tile, lane):
    return jnp.broadcast_to(tile[:, lane:lane + 1], tile.shape)


def row_spread(tile, row):
    return jnp.broadcast_to(tile[row:row + 1, :], tile.shape)


def eliminate_block(block):
    strips = BLK // SUB
    sub = lax.broadcasted_iota(jnp.int32, (SUB, BLK), 0)
    lane = lax.broadcasted_iota(jnp.int32, (SUB, BLK), 1)
    upper = [block[SUB * s:SUB * s + SUB, :] for s in range(strips)]
    lower = [jnp.where(lane == sub + SUB * s, 1.0, 0.0) for s in range(strips)]
    pivots = []
    for p in range(strips):
        first = SUB * p
        cols = [lane_spread(upper[p], first + j) for j in range(SUB)]
        a, x = upper[p], lower[p]
        recips = []
        pivot = jnp.zeros((SUB, BLK), jnp.float32)
        for j in range(SUB):
            d = row_spread(cols[j], j)
            recip = 1.0 / d
            recips.append(recip)
            pivot = jnp.where(sub == j, d, pivot)
            if j + 1 < SUB:
                m = jnp.where(sub > j, cols[j] * recip, 0.0)
                for k in range(j + 1, SUB):
                    cols[k] = cols[k] - m * row_spread(cols[k], j)
                a = a - m * row_spread(a, j)
                x = x - m * row_spread(x, j)
        upper[p], lower[p] = a, x
        pivots.append(pivot)
        if p + 1 == strips:
            break
        va = [row_spread(a, j) * recips[j] for j in range(SUB)]
        vx = [row_spread(x, j) * recips[j] for j in range(SUB)]
        for j in range(SUB - 2, -1, -1):
            for k in range(j + 1, SUB):
                c = row_spread(cols[k], j) * recips[j]
                va[j] = va[j] - c * va[k]
                vx[j] = vx[j] - c * vx[k]
        for s in range(p + 1, strips):
            b = [lane_spread(upper[s], first + j) for j in range(SUB)]
            upper[s] = upper[s] - (
                ((b[0] * va[0] + b[1] * va[1]) + (b[2] * va[2] + b[3] * va[3]))
                + ((b[4] * va[4] + b[5] * va[5]) + (b[6] * va[6] + b[7] * va[7]))
            )
            lower[s] = lower[s] - (
                ((b[0] * vx[0] + b[1] * vx[1]) + (b[2] * vx[2] + b[3] * vx[3]))
                + ((b[4] * vx[4] + b[5] * vx[5]) + (b[6] * vx[6] + b[7] * vx[7]))
            )
    return (
        jnp.concatenate(upper, axis=0),
        jnp.concatenate(lower, axis=0),
        jnp.concatenate(pivots, axis=0),
    )


def exact_dot(a, b, dims=((1,), (0,))):
    return lax.dot_general(
        a, b, (dims, ((), ())),
        precision=lax.Precision.HIGHEST,
        preferred_element_type=jnp.float32,
    )


def vmem_specs(count):
    return [pl.BlockSpec(memory_space=pltpu.VMEM)] * count


def pivot_rows_kernel(place, blocks, front_hbm, child_hbm, out_ref, front_ref, child_ref, sems):
    front = pltpu.make_async_copy(front_hbm.at[:S, :], front_ref, sems.at[0])
    child = pltpu.make_async_copy(child_hbm.at[:S, :], child_ref, sems.at[1])
    front.start()
    child.start()
    front.wait()
    child.wait()
    for b in range(S // BLK):
        rows = slice(b * BLK, (b + 1) * BLK)
        total = jnp.where(place[1] == 0, front_ref[rows, :], 0.0)
        for k in range(b + 1):
            total += jnp.where(blocks[k] == b, child_ref[k * BLK:(k + 1) * BLK, :], 0.0)
        out_ref[rows, :] = total


def pivot_rows(place, blocks, front, child):
    cc = front.shape[1]
    smem = pl.BlockSpec(memory_space=pltpu.SMEM)
    hbm = pl.BlockSpec(memory_space=pl.ANY)
    return pl.pallas_call(
        pivot_rows_kernel,
        out_shape=jax.ShapeDtypeStruct((S, cc), jnp.float32),
        in_specs=[smem, smem, hbm, hbm],
        out_specs=pl.BlockSpec(memory_space=pltpu.VMEM),
        scratch_shapes=[pltpu.VMEM((S, cc), jnp.float32)] * 2
        + [pltpu.SemaphoreType.DMA((2,))],
        compiler_params=pltpu.CompilerParams(vmem_limit_bytes=56 * MIB),
        cost_estimate=pl.CostEstimate(
            flops=4 * S * cc, bytes_accessed=12 * S * cc, transcendentals=0),
        name="pivot_rows",
    )(place, blocks, front, child)


def child_rows_kernel(pieces, leaf, child_hbm, out_hbm, sems):
    rows = out_hbm.shape[0]
    size = rows // pieces
    first = (1 - leaf[0]) * (child_hbm.shape[0] - rows)

    def copy(n):
        start = pl.multiple_of(first + n * size, BLK)
        return pltpu.make_async_copy(
            child_hbm.at[pl.ds(start, size), :], out_hbm.at[n * size:(n + 1) * size, :], sems.at[n])

    for n in range(pieces):
        copy(n).start()
    for n in range(pieces):
        copy(n).wait()


def child_rows(leaf, child, rows):
    pieces = 8
    hbm = pl.BlockSpec(memory_space=pl.ANY)
    return pl.pallas_call(
        functools.partial(child_rows_kernel, pieces),
        out_shape=jax.ShapeDtypeStruct((rows, child.shape[1]), jnp.float32),
        in_specs=[pl.BlockSpec(memory_space=pltpu.SMEM), hbm],
        out_specs=hbm,
        scratch_shapes=[pltpu.SemaphoreType.DMA((pieces,))],
        compiler_params=pltpu.CompilerParams(vmem_limit_bytes=56 * MIB),
        cost_estimate=pl.CostEstimate(flops=0, bytes_accessed=4 * S, transcendentals=0),
        name="child_rows",
    )(leaf.reshape(1), child)


def packed_blocks():
    count = S // BLK
    order = [(i, j) for i in range(count) for j in range(i, count)]
    return order[:len(order) // 2], order[len(order) // 2:]


def block_slices(block):
    i, j = block
    return slice(i * BLK, (i + 1) * BLK), slice(j * BLK, (j + 1) * BLK)


def pivot_sum_kernel(place, mine_ref, other_ref, cols_ref, piece_ref, *packed):
    cols = mine_ref[...] + other_ref[...]
    cols_ref[...] = cols
    piece_ref[...] = cols.T
    if packed:
        size = packed[0].shape[0]
        for n, blocks in enumerate(zip(*packed_blocks())):
            low, high = (cols[block_slices(block)] for block in blocks)
            value = jnp.where(place[1] == 0, low, high)
            value = jnp.where(place[0] == 0, value, 0.0)
            for ref, start in zip(packed, (0, size)):
                begin = max(n * BLK, start)
                end = min((n + 1) * BLK, start + size)
                if begin < end:
                    ref[begin - start:end - start, :] = value[begin - n * BLK:end - n * BLK]


def pivot_sum(place, mine, other):
    cc = mine.shape[1]
    shapes = [(S, cc), (cc, S)]
    if cc == S:
        shapes += [(len(packed_blocks()[0]) * BLK // 2, BLK)] * 2
    return pl.pallas_call(
        pivot_sum_kernel,
        out_shape=[jax.ShapeDtypeStruct(shape, jnp.float32) for shape in shapes],
        in_specs=[pl.BlockSpec(memory_space=pltpu.SMEM)] + vmem_specs(2),
        out_specs=vmem_specs(len(shapes)),
        compiler_params=pltpu.CompilerParams(vmem_limit_bytes=16 * MIB),
        cost_estimate=pl.CostEstimate(
            flops=S * cc, bytes_accessed=16 * S * cc, transcendentals=0),
        name="pivot_sum",
    )(place, mine, other)


def choose_kernel(own, piece_ref, came_ref, out_ref):
    out_ref[...] = jnp.where(own[0] > 0, piece_ref[...], came_ref[...])


def choose(own, piece, came):
    return pl.pallas_call(
        choose_kernel,
        out_shape=jax.ShapeDtypeStruct(piece.shape, jnp.float32),
        in_specs=[pl.BlockSpec(memory_space=pltpu.SMEM)] + vmem_specs(2),
        out_specs=pl.BlockSpec(memory_space=pltpu.VMEM),
        compiler_params=pltpu.CompilerParams(vmem_limit_bytes=56 * MIB),
        cost_estimate=pl.CostEstimate(flops=S, bytes_accessed=4 * S, transcendentals=0),
        name="choose",
    )(own.astype(jnp.int32).reshape(1), piece, came)


def factor_step(step, u_ref, x_ref):
    rows = slice(step * BLK, (step + 1) * BLK)
    done, rest = slice(0, (step + 1) * BLK), slice((step + 1) * BLK, S)
    block, inverse, pivots = eliminate_block(u_ref[rows, rows])
    scale = lax.rsqrt(pivots)
    scale = scale * (1.5 - 0.5 * pivots * scale * scale)
    r = lax.broadcasted_iota(jnp.int32, (BLK, BLK), 0)
    c = lax.broadcasted_iota(jnp.int32, (BLK, BLK), 1)
    u_ref[rows, rows] = jnp.where(c >= r, block * scale, 0.0)
    inverse = inverse * scale
    x = exact_dot(inverse, x_ref[rows, done])
    x_ref[rows, done] = x
    if step:
        u_ref[rows, :step * BLK] = jnp.zeros((BLK, step * BLK), jnp.float32)
    if step + 1 < S // BLK:
        u = exact_dot(inverse, u_ref[rows, rest])
        u_ref[rows, rest] = u
        u_ref[rest, rest] -= exact_dot(u, u, ((0,), (0,)))
        x_ref[rest, done] -= exact_dot(u, x, ((0,), (0,)))


def first_step_kernel(place, *refs):
    u_ref, x_ref = refs[-2:]
    sources = refs[:-2]
    if len(sources) == 1:
        u_ref[...] = sources[0][...]
    else:
        mine = jnp.concatenate([ref[...] for ref in sources[:2]], axis=0)
        other = jnp.concatenate([ref[...] for ref in sources[2:]], axis=0)
        values = [
            jnp.where(place[1] == 0, mine, other), jnp.where(place[1] == 0, other, mine)]
        for value, blocks in zip(values, packed_blocks()):
            for n, block in enumerate(blocks):
                u_ref[block_slices(block)] = value[n * BLK:(n + 1) * BLK]
    eye = lax.broadcasted_iota(jnp.int32, (S, S), 0) == lax.broadcasted_iota(
        jnp.int32, (S, S), 1)
    x_ref[...] = jnp.where(eye, 1.0, 0.0)
    factor_step(0, u_ref, x_ref)


def middle_step_kernel(step, u_in, x_in, u_ref, x_ref):
    u_ref[...] = u_in[...]
    x_ref[...] = x_in[...]
    factor_step(step, u_ref, x_ref)


def last_step_kernel(place, u_in, x_in, cols_ref, top_ref, mult_ref, u_ref, x_ref):
    u_ref[...] = u_in[...]
    x_ref[...] = x_in[...]
    factor_step(S // BLK - 1, u_ref, x_ref)
    cc = cols_ref.shape[1]
    is_pivot = place[0] < S // cc
    start = pl.multiple_of(jnp.minimum(place[0], S // cc - 1) * cc, cc)
    solved = exact_dot(x_ref[...], cols_ref[...])
    top_ref[...] = jnp.where(is_pivot, u_ref[pl.ds(start, cc), :].T, solved)
    unit = lax.broadcasted_iota(jnp.int32, (S, cc), 0) == start + lax.broadcasted_iota(
        jnp.int32, (S, cc), 1)
    right = jnp.where(is_pivot, jnp.where(unit, -1.0, 0.0), solved)
    mult_ref[...] = exact_dot(x_ref[...], right, ((0,), (0,)))


FACTOR_PARAMS = dict(
    compiler_params=pltpu.CompilerParams(vmem_limit_bytes=48 * MIB),
    cost_estimate=pl.CostEstimate(
        flops=10 ** 6, bytes_accessed=4 * S, transcendentals=0),
)
SQUARE = jax.ShapeDtypeStruct((S, S), jnp.float32)


def first_step(place, sources):
    return pl.pallas_call(
        first_step_kernel,
        out_shape=[SQUARE] * 2,
        in_specs=[pl.BlockSpec(memory_space=pltpu.SMEM)] + vmem_specs(len(sources)),
        out_specs=vmem_specs(2),
        name="factor_step",
        **FACTOR_PARAMS,
    )(place, *sources)


def middle_step(step, u, x):
    return pl.pallas_call(
        functools.partial(middle_step_kernel, step),
        out_shape=[SQUARE] * 2,
        in_specs=vmem_specs(2),
        out_specs=vmem_specs(2),
        name="factor_step",
        **FACTOR_PARAMS,
    )(u, x)


def last_step(place, u, x, cols):
    return pl.pallas_call(
        last_step_kernel,
        out_shape=[jax.ShapeDtypeStruct(cols.shape, jnp.float32)] * 2,
        in_specs=[pl.BlockSpec(memory_space=pltpu.SMEM)] + vmem_specs(3),
        out_specs=vmem_specs(2),
        scratch_shapes=[pltpu.VMEM((S, S), jnp.float32)] * 2,
        name="factor_and_solve",
        **FACTOR_PARAMS,
    )(place, u, x, cols)


GROUP = 4


def assemble_kernel(
        index, front_hbm, child_hbm, recv_hbm, out_hbm, rows_ref, own_ref, recv_ref, *sems):
    front_sems, own_sems, recv_sems, out_sems = sems
    count = rows_ref.shape[0]
    size = GROUP * BLK

    def front_copy(n):
        return pltpu.make_async_copy(
            front_hbm.at[n * size:(n + 1) * size, :], rows_ref.at[n], front_sems.at[n])

    def own_copy(block):
        start = pl.multiple_of(index[0, block] * BLK, BLK)
        return pltpu.make_async_copy(
            child_hbm.at[pl.ds(start, BLK), :], own_ref.at[block], own_sems.at[block])

    def recv_copy(block):
        start = pl.multiple_of(index[2, block] * BLK, BLK)
        return pltpu.make_async_copy(
            recv_hbm.at[pl.ds(start, BLK), :], recv_ref.at[block], recv_sems.at[block])

    def out_copy(n):
        return pltpu.make_async_copy(
            rows_ref.at[n], out_hbm.at[n * size:(n + 1) * size, :], out_sems.at[n])

    for n in range(count):
        front_copy(n).start()
        for j in range(GROUP):
            own_copy(n * GROUP + j).start()
            recv_copy(n * GROUP + j).start()
    for n in range(count):
        front_copy(n).wait()
        for j in range(GROUP):
            block = n * GROUP + j
            own_copy(block).wait()
            recv_copy(block).wait()
            rows = slice(j * BLK, (j + 1) * BLK)
            own = jnp.where(index[1, block] > 0, own_ref[block], 0.0)
            recv = jnp.where(index[3, block] > 0, recv_ref[block], 0.0)
            rows_ref[n, rows, :] = rows_ref[n, rows, :] + own + recv
        out_copy(n).start()
    for n in range(count):
        out_copy(n).wait()


def assemble(index, front, child, recv):
    rows, cc = front.shape
    blocks = rows // BLK
    count = blocks // GROUP
    hbm = pl.BlockSpec(memory_space=pl.ANY)
    return pl.pallas_call(
        assemble_kernel,
        out_shape=jax.ShapeDtypeStruct((rows, cc), jnp.float32),
        in_specs=[pl.BlockSpec(memory_space=pltpu.SMEM), hbm, hbm, hbm],
        out_specs=hbm,
        scratch_shapes=[
            pltpu.VMEM((count, GROUP * BLK, cc), jnp.float32),
            pltpu.VMEM((blocks, BLK, cc), jnp.float32),
            pltpu.VMEM((blocks, BLK, cc), jnp.float32),
            pltpu.SemaphoreType.DMA((count,)),
            pltpu.SemaphoreType.DMA((blocks,)),
            pltpu.SemaphoreType.DMA((blocks,)),
            pltpu.SemaphoreType.DMA((count,)),
        ],
        compiler_params=pltpu.CompilerParams(vmem_limit_bytes=48 * MIB),
        cost_estimate=pl.CostEstimate(
            flops=2 * rows, bytes_accessed=16 * rows, transcendentals=0),
        name="assemble",
    )(index, front, child, recv)


def finish_kernel(parts, place, base_hbm, mult_ref, top_ref, *refs):
    pieces, refs = refs[:len(parts)], refs[len(parts):]
    out_hbm, rows_ref, piece_ref, in_sems, piece_sems, out_sems = refs
    cc = mult_ref.shape[1]
    is_pivot = place[0] < S // cc

    def start_of(n):
        slot, first, _ = parts[n]
        return pl.multiple_of(jnp.bitwise_xor(place[2], slot) * cc + first, parts[n][2])

    def held(ref, n):
        return ref.at[n, pl.ds(0, parts[n][2]), :]

    def rows_of(n):
        return pl.ds(start_of(n), parts[n][2])

    def base_copy(n):
        return pltpu.make_async_copy(base_hbm.at[rows_of(n), :], held(rows_ref, n), in_sems.at[n])

    def piece_copy(n):
        return pltpu.make_async_copy(pieces[n], held(piece_ref, n), piece_sems.at[n])

    def out_copy(n):
        return pltpu.make_async_copy(held(rows_ref, n), out_hbm.at[rows_of(n), :], out_sems.at[n])

    for n in range(len(parts)):
        piece_copy(n).start()
        base_copy(n).start()
    for n in range(len(parts)):
        piece_copy(n).wait()
        base_copy(n).wait()
        is_top = jnp.logical_and(place[1] == 0, start_of(n) < S)

        @pl.when(is_top)
        def _():
            held(rows_ref, n)[...] = top_ref[rows_of(n), :]

        @pl.when(jnp.logical_not(is_top))
        def _():
            product = lax.dot_general(
                held(piece_ref, n)[...], mult_ref[...], (((1,), (0,)), ((), ())),
                precision=lax.Precision.HIGH,
                preferred_element_type=jnp.float32,
            )
            held(rows_ref, n)[...] = jnp.where(is_pivot, 0.0, held(rows_ref, n)[...]) - product

        out_copy(n).start()
    for n in range(len(parts)):
        out_copy(n).wait()


def finish(place, base, parts, mult, top):
    rows, cc = base.shape
    count = len(parts)
    total = sum(piece.shape[0] for _, _, piece in parts)
    hbm = pl.BlockSpec(memory_space=pl.ANY)
    keys = tuple((slot, first, piece.shape[0]) for slot, first, piece in parts)
    return pl.pallas_call(
        functools.partial(finish_kernel, keys),
        out_shape=jax.ShapeDtypeStruct((rows, cc), jnp.float32),
        in_specs=[pl.BlockSpec(memory_space=pltpu.SMEM), hbm] + vmem_specs(2) + [hbm] * count,
        out_specs=hbm,
        scratch_shapes=[
            pltpu.VMEM((count, cc, cc), jnp.float32),
            pltpu.VMEM((count, cc, S), jnp.float32),
        ]
        + [pltpu.SemaphoreType.DMA((count,))] * 3,
        input_output_aliases={1: 0},
        compiler_params=pltpu.CompilerParams(vmem_limit_bytes=48 * MIB),
        cost_estimate=pl.CostEstimate(
            flops=6 * total * S * cc, bytes_accessed=4 * total * (2 * cc + S),
            transcendentals=0),
        name="finish",
    )(place, base, mult, top, *[piece for _, _, piece in parts])


def block_places(blocks, first, count, shift, limit):
    parent = first + jnp.arange(count, dtype=jnp.int32)
    reached = jnp.sum((blocks[None, :] <= parent[:, None]).astype(jnp.int32), axis=1)
    there = jnp.sum((blocks[None, :] == parent[:, None]).astype(jnp.int32), axis=1)
    return jnp.clip(reached - 1 - shift, 0, limit - 1), there


def spread_pivot(cols, front_index, front_count, holders):
    leaf_index = lax.axis_index("leaf")
    half = S // 2
    mine = lax.dynamic_slice_in_dim(cols, leaf_index * half, half, 0)
    steps = []
    step = holders
    while step < front_count:
        steps.append(step)
        step *= 2
    pieces = []
    for order, part in ((steps, mine[:half // 2]), (steps[::-1], mine[half // 2:])):
        held = list(range(holders))
        part = jnp.where(front_index < holders, part, 0.0)
        for step in order:
            got = lax.ppermute(part, "front", [(f, f + step) for f in held])
            part = part + got
            held += [f + step for f in held]
        pieces.append(part)
    mine = jnp.concatenate(pieces, axis=0)
    if holders > 1:
        groups = [list(range(f, f + holders)) for f in range(0, front_count, holders)]
        mine = lax.all_gather(mine, "front", axis_index_groups=groups, axis=1, tiled=True)
    other = lax.ppermute(mine, "leaf", [(0, 1), (1, 0)])
    low = jnp.where(leaf_index == 0, mine, other)
    high = jnp.where(leaf_index == 0, other, mine)
    return jnp.concatenate([low, high], axis=0)


def pass_on(part, steps, n):
    held = [0]
    for step in steps[:n]:
        held += [f + step for f in held]
    return part + lax.ppermute(part, "front", [(f, f + steps[n]) for f in held])


def per_device(front_block, child_update, child_map):
    row_count, col_count = front_block.shape
    front_count = lax.axis_size("front")
    leaf_index = lax.axis_index("leaf")
    front_index = lax.axis_index("front")
    half = front_count // 2
    place = jnp.stack([front_index, leaf_index, front_index % half]).astype(jnp.int32)
    swap = [(0, 1), (1, 0)]
    child = child_update[0]
    blocks = child_map[0]
    child_blocks = blocks.shape[0]
    parent_blocks = row_count // BLK

    mine = pivot_rows(place, blocks, front_block, child)
    cols, piece, *packed = pivot_sum(place, mine, lax.ppermute(mine, "leaf", swap))

    pairs = [(f, f + half) for f in range(half)]
    pairs += [(front_count + f + half, front_count + f) for f in range(half)]
    came = lax.ppermute(piece, ("leaf", "front"), pairs)

    other_blocks = lax.ppermute(blocks, "leaf", swap)
    first = leaf_index * parent_blocks
    shift = leaf_index * (child_blocks - parent_blocks)
    index = jnp.stack(
        block_places(blocks, first, parent_blocks, 0, child_blocks)
        + block_places(other_blocks, first, parent_blocks, shift, parent_blocks))

    def across(value, bit):
        return lax.ppermute(value, "front", [(f, f ^ bit) for f in range(front_count)])

    barrier = lax.optimization_barrier
    own = (front_index >= half) == (leaf_index == 1)
    if packed:
        orders, step = [[1, 2], [2, 1]], 4
        while step <= half:
            for order in orders:
                order.append(step)
            step *= 2
        parts = [pass_on(part, order, 0) for part, order in zip(packed, orders)]
        parts, later = barrier((parts, leaf_index))
        sent = child_rows(later, child, row_count)
        parts = [pass_on(part, order, 1) for part, order in zip(parts, orders)]
        parts, sent, index, came = barrier((parts, sent, index, came))
        recv = lax.ppermute(sent, "leaf", swap)
        for n in range(2, len(orders[0]) - 1):
            parts = barrier([pass_on(part, order, n) for part, order in zip(parts, orders)])
    else:
        recv = lax.ppermute(child_rows(leaf_index, child, row_count), "leaf", swap)
        sources = [spread_pivot(cols, front_index, front_count, S // col_count)]
    piece = choose(own, piece, came)

    bit, slots, held = half // 2, [0], [piece]
    while bit > 4:
        held += [across(part, bit) for part in held]
        slots += [slot + bit for slot in slots]
        bit //= 2
    sides = [(across(part, 1), across(part, 2)) for part in held]
    if packed:
        parts = [pass_on(part, order, len(order) - 1) for part, order in zip(parts, orders)]
        parts, recv, held = barrier((parts, recv, held))
        sources = parts + [lax.ppermute(part, "leaf", swap) for part in parts]
    over = [across(part, 4) for part in held]
    out = assemble(index, front_block, child, recv)
    sources, out, sides = barrier((sources, out, sides))
    cut = col_count // 2
    crossed = [(across(xs[:cut], 2), across(ys[cut:], 1)) for xs, ys in sides]
    u, x = first_step(place, sources)
    u, x, over = barrier((u, x, over))
    over_sides = [(across(part, 1), across(part, 2)) for part in over]
    u, x = middle_step(1, u, x)
    u, x, crossed = barrier((u, x, crossed))
    over_crossed = [(across(low, 4), across(high, 4)) for low, high in crossed]
    u, x = middle_step(2, u, x)
    top, mult = last_step(place, u, x, cols)

    early, late = [], []
    for group, first, alone, beside, cross in (
            (early, 0, held, sides, crossed), (late, 4, over, over_sides, over_crossed)):
        for slot, part, (xs, ys), (low, high) in zip(slots, alone, beside, cross):
            slot += first
            early.append((slot, 0, part))
            group += [(slot + 1, 0, xs), (slot + 2, 0, ys)]
            group += [(slot + 3, 0, low), (slot + 3, cut, high)]
    for group in (early, late):
        out = finish(place, out, group, mult, top)
    return out


def solution(mesh):
    return jax.shard_map(
        per_device,
        mesh=mesh,
        in_specs=(P("leaf", "front"), P("leaf", None, "front"), P("leaf", None)),
        out_specs=P("leaf", "front"),
        check_vma=False,
    )
```

```python
import functools

import jax
import jax.numpy as jnp
from jax import lax
from jax.experimental import pallas as pl
from jax.experimental.pallas import tpu as pltpu
from jax.sharding import PartitionSpec as P

BLK = 128
S = 512
SUB = 8
MIB = 1024 * 1024


def lane_spread(tile, lane):
    return jnp.broadcast_to(tile[:, lane:lane + 1], tile.shape)


def row_spread(tile, row):
    return jnp.broadcast_to(tile[row:row + 1, :], tile.shape)


def eliminate_block(block):
    strips = BLK // SUB
    sub = lax.broadcasted_iota(jnp.int32, (SUB, BLK), 0)
    lane = lax.broadcasted_iota(jnp.int32, (SUB, BLK), 1)
    upper = [block[SUB * s:SUB * s + SUB, :] for s in range(strips)]
    lower = [jnp.where(lane == sub + SUB * s, 1.0, 0.0) for s in range(strips)]
    pivots = []
    for p in range(strips):
        first = SUB * p
        cols = [lane_spread(upper[p], first + j) for j in range(SUB)]
        a, x = upper[p], lower[p]
        recips = []
        pivot = jnp.zeros((SUB, BLK), jnp.float32)
        for j in range(SUB):
            d = row_spread(cols[j], j)
            recip = 1.0 / d
            recips.append(recip)
            pivot = jnp.where(sub == j, d, pivot)
            if j + 1 < SUB:
                m = jnp.where(sub > j, cols[j] * recip, 0.0)
                for k in range(j + 1, SUB):
                    cols[k] = cols[k] - m * row_spread(cols[k], j)
                a = a - m * row_spread(a, j)
                x = x - m * row_spread(x, j)
        upper[p], lower[p] = a, x
        pivots.append(pivot)
        if p + 1 == strips:
            break
        va = [row_spread(a, j) * recips[j] for j in range(SUB)]
        vx = [row_spread(x, j) * recips[j] for j in range(SUB)]
        for j in range(SUB - 2, -1, -1):
            for k in range(j + 1, SUB):
                c = row_spread(cols[k], j) * recips[j]
                va[j] = va[j] - c * va[k]
                vx[j] = vx[j] - c * vx[k]
        for s in range(p + 1, strips):
            b = [lane_spread(upper[s], first + j) for j in range(SUB)]
            upper[s] = upper[s] - (
                ((b[0] * va[0] + b[1] * va[1]) + (b[2] * va[2] + b[3] * va[3]))
                + ((b[4] * va[4] + b[5] * va[5]) + (b[6] * va[6] + b[7] * va[7]))
            )
            lower[s] = lower[s] - (
                ((b[0] * vx[0] + b[1] * vx[1]) + (b[2] * vx[2] + b[3] * vx[3]))
                + ((b[4] * vx[4] + b[5] * vx[5]) + (b[6] * vx[6] + b[7] * vx[7]))
            )
    return (
        jnp.concatenate(upper, axis=0),
        jnp.concatenate(lower, axis=0),
        jnp.concatenate(pivots, axis=0),
    )


def exact_dot(a, b, dims=((1,), (0,))):
    return lax.dot_general(
        a, b, (dims, ((), ())),
        precision=lax.Precision.HIGHEST,
        preferred_element_type=jnp.float32,
    )


def vmem_specs(count):
    return [pl.BlockSpec(memory_space=pltpu.VMEM)] * count


def pivot_rows_kernel(place, blocks, front_hbm, child_hbm, out_ref, front_ref, child_ref, sems):
    def copies(b):
        rows = slice(b * BLK, (b + 1) * BLK)
        return [
            pltpu.make_async_copy(hbm.at[rows, :], ref.at[rows, :], sems.at[n, b])
            for n, (hbm, ref) in enumerate(((front_hbm, front_ref), (child_hbm, child_ref)))]

    waits = [copies(b) for b in range(S // BLK)]
    for pair in waits:
        for copy in pair:
            copy.start()
    for b in range(S // BLK):
        for copy in waits[b]:
            copy.wait()
        rows = slice(b * BLK, (b + 1) * BLK)
        total = jnp.where(place[1] == 0, front_ref[rows, :], 0.0)
        for k in range(b + 1):
            total += jnp.where(blocks[k] == b, child_ref[k * BLK:(k + 1) * BLK, :], 0.0)
        out_ref[rows, :] = total


def pivot_rows(place, blocks, front, child):
    cc = front.shape[1]
    smem = pl.BlockSpec(memory_space=pltpu.SMEM)
    hbm = pl.BlockSpec(memory_space=pl.ANY)
    return pl.pallas_call(
        pivot_rows_kernel,
        out_shape=jax.ShapeDtypeStruct((S, cc), jnp.float32),
        in_specs=[smem, smem, hbm, hbm],
        out_specs=pl.BlockSpec(memory_space=pltpu.VMEM),
        scratch_shapes=[pltpu.VMEM((S, cc), jnp.float32)] * 2
        + [pltpu.SemaphoreType.DMA((2, S // BLK))],
        compiler_params=pltpu.CompilerParams(vmem_limit_bytes=54 * MIB),
        cost_estimate=pl.CostEstimate(
            flops=4 * S * cc, bytes_accessed=12 * S * cc, transcendentals=0),
        name="pivot_rows",
    )(place, blocks, front, child)


def child_rows_kernel(pieces, leaf, child_hbm, out_hbm, rows_ref, in_sems, out_sems):
    rows = out_hbm.shape[0]
    size = rows // pieces
    first = (1 - leaf[0]) * (child_hbm.shape[0] - rows)

    def in_copy(n):
        start = pl.multiple_of(first + n * size, BLK)
        return pltpu.make_async_copy(
            child_hbm.at[pl.ds(start, size), :], rows_ref.at[n], in_sems.at[n])

    def out_copy(n):
        return pltpu.make_async_copy(
            rows_ref.at[n], out_hbm.at[n * size:(n + 1) * size, :], out_sems.at[n])

    for n in range(pieces):
        in_copy(n).start()
    for n in range(pieces):
        in_copy(n).wait()
        out_copy(n).start()
    for n in range(pieces):
        out_copy(n).wait()


def child_rows(leaf, child, rows):
    pieces = 8
    hbm = pl.BlockSpec(memory_space=pl.ANY)
    return pl.pallas_call(
        functools.partial(child_rows_kernel, pieces),
        out_shape=jax.ShapeDtypeStruct((rows, child.shape[1]), jnp.float32),
        in_specs=[pl.BlockSpec(memory_space=pltpu.SMEM), hbm],
        out_specs=hbm,
        scratch_shapes=[pltpu.VMEM((pieces, rows // pieces, child.shape[1]), jnp.float32)]
        + [pltpu.SemaphoreType.DMA((pieces,))] * 2,
        compiler_params=pltpu.CompilerParams(vmem_limit_bytes=56 * MIB),
        cost_estimate=pl.CostEstimate(flops=0, bytes_accessed=4 * S, transcendentals=0),
        name="child_rows",
    )(leaf.reshape(1), child)


def packed_blocks():
    count = S // BLK
    order = [(i, j) for i in range(count) for j in range(i, count)]
    return order[:len(order) // 2], order[len(order) // 2:]


def block_slices(block):
    i, j = block
    return slice(i * BLK, (i + 1) * BLK), slice(j * BLK, (j + 1) * BLK)


def pivot_sum_kernel(place, mine_ref, other_ref, cols_ref, piece_ref, *packed):
    cols = mine_ref[...] + other_ref[...]
    cols_ref[...] = cols
    piece_ref[...] = cols.T
    if packed:
        size = packed[0].shape[0]
        for n, blocks in enumerate(zip(*packed_blocks())):
            low, high = (cols[block_slices(block)] for block in blocks)
            value = jnp.where(place[1] == 0, low, high)
            value = jnp.where(place[0] == 0, value, 0.0)
            for ref, start in zip(packed, (0, size)):
                begin = max(n * BLK, start)
                end = min((n + 1) * BLK, start + size)
                if begin < end:
                    ref[begin - start:end - start, :] = value[begin - n * BLK:end - n * BLK]


def pivot_sum(place, mine, other):
    cc = mine.shape[1]
    shapes = [(S, cc), (cc, S)]
    if cc == S:
        shapes += [(len(packed_blocks()[0]) * BLK // 2, BLK)] * 2
    return pl.pallas_call(
        pivot_sum_kernel,
        out_shape=[jax.ShapeDtypeStruct(shape, jnp.float32) for shape in shapes],
        in_specs=[pl.BlockSpec(memory_space=pltpu.SMEM)] + vmem_specs(2),
        out_specs=vmem_specs(len(shapes)),
        compiler_params=pltpu.CompilerParams(vmem_limit_bytes=16 * MIB),
        cost_estimate=pl.CostEstimate(
            flops=S * cc, bytes_accessed=16 * S * cc, transcendentals=0),
        name="pivot_sum",
    )(place, mine, other)


def factor_step(step, u_ref, x_ref):
    rows = slice(step * BLK, (step + 1) * BLK)
    done, rest = slice(0, (step + 1) * BLK), slice((step + 1) * BLK, S)
    block, inverse, pivots = eliminate_block(u_ref[rows, rows])
    scale = lax.rsqrt(pivots)
    scale = scale * (1.5 - 0.5 * pivots * scale * scale)
    r = lax.broadcasted_iota(jnp.int32, (BLK, BLK), 0)
    c = lax.broadcasted_iota(jnp.int32, (BLK, BLK), 1)
    u_ref[rows, rows] = jnp.where(c >= r, block * scale, 0.0)
    inverse = inverse * scale
    x = exact_dot(inverse, x_ref[rows, done])
    x_ref[rows, done] = x
    if step:
        u_ref[rows, :step * BLK] = jnp.zeros((BLK, step * BLK), jnp.float32)
    if step + 1 < S // BLK:
        u = exact_dot(inverse, u_ref[rows, rest])
        u_ref[rows, rest] = u
        u_ref[rest, rest] -= exact_dot(u, u, ((0,), (0,)))
        x_ref[rest, done] -= exact_dot(u, x, ((0,), (0,)))


def first_step_kernel(place, *refs):
    u_ref, x_ref = refs[-2:]
    sources = refs[:-2]
    if len(sources) == 1:
        u_ref[...] = sources[0][...]
    else:
        mine = jnp.concatenate([ref[...] for ref in sources[:2]], axis=0)
        other = jnp.concatenate([ref[...] for ref in sources[2:]], axis=0)
        values = [
            jnp.where(place[1] == 0, mine, other), jnp.where(place[1] == 0, other, mine)]
        for value, blocks in zip(values, packed_blocks()):
            for n, block in enumerate(blocks):
                u_ref[block_slices(block)] = value[n * BLK:(n + 1) * BLK]
    eye = lax.broadcasted_iota(jnp.int32, (S, S), 0) == lax.broadcasted_iota(
        jnp.int32, (S, S), 1)
    x_ref[...] = jnp.where(eye, 1.0, 0.0)
    factor_step(0, u_ref, x_ref)


def middle_step_kernel(step, u_in, x_in, u_ref, x_ref):
    u_ref[...] = u_in[...]
    x_ref[...] = x_in[...]
    factor_step(step, u_ref, x_ref)


def last_step_kernel(place, u_in, x_in, cols_ref, top_ref, mult_ref, u_ref, x_ref):
    u_ref[...] = u_in[...]
    x_ref[...] = x_in[...]
    factor_step(S // BLK - 1, u_ref, x_ref)
    cc = cols_ref.shape[1]
    is_pivot = place[0] < S // cc
    start = pl.multiple_of(jnp.minimum(place[0], S // cc - 1) * cc, cc)
    solved = exact_dot(x_ref[...], cols_ref[...])
    top_ref[...] = jnp.where(is_pivot, u_ref[pl.ds(start, cc), :].T, solved)
    unit = lax.broadcasted_iota(jnp.int32, (S, cc), 0) == start + lax.broadcasted_iota(
        jnp.int32, (S, cc), 1)
    right = jnp.where(is_pivot, jnp.where(unit, -1.0, 0.0), solved)
    mult_ref[...] = exact_dot(x_ref[...], right, ((0,), (0,)))


FACTOR_PARAMS = dict(
    compiler_params=pltpu.CompilerParams(vmem_limit_bytes=48 * MIB),
    cost_estimate=pl.CostEstimate(
        flops=10 ** 6, bytes_accessed=4 * S, transcendentals=0),
)
SQUARE = jax.ShapeDtypeStruct((S, S), jnp.float32)


def first_step(place, sources):
    return pl.pallas_call(
        first_step_kernel,
        out_shape=[SQUARE] * 2,
        in_specs=[pl.BlockSpec(memory_space=pltpu.SMEM)] + vmem_specs(len(sources)),
        out_specs=vmem_specs(2),
        name="factor_step",
        **FACTOR_PARAMS,
    )(place, *sources)


def middle_step(step, u, x):
    return pl.pallas_call(
        functools.partial(middle_step_kernel, step),
        out_shape=[SQUARE] * 2,
        in_specs=vmem_specs(2),
        out_specs=vmem_specs(2),
        name="factor_step",
        **FACTOR_PARAMS,
    )(u, x)


def last_step(place, u, x, cols):
    return pl.pallas_call(
        last_step_kernel,
        out_shape=[jax.ShapeDtypeStruct(cols.shape, jnp.float32)] * 2,
        in_specs=[pl.BlockSpec(memory_space=pltpu.SMEM)] + vmem_specs(3),
        out_specs=vmem_specs(2),
        scratch_shapes=[pltpu.VMEM((S, S), jnp.float32)] * 2,
        name="factor_and_solve",
        **FACTOR_PARAMS,
    )(place, u, x, cols)


GROUP = 4


def assemble_kernel(index, front_hbm, child_hbm, out_hbm, rows_ref, own_ref, *sems):
    front_sems, own_sems, out_sems = sems
    count = rows_ref.shape[0]
    size = GROUP * BLK

    def front_copy(n):
        return pltpu.make_async_copy(
            front_hbm.at[n * size:(n + 1) * size, :], rows_ref.at[n], front_sems.at[n])

    def own_copy(block):
        start = pl.multiple_of(index[0, block] * BLK, BLK)
        return pltpu.make_async_copy(
            child_hbm.at[pl.ds(start, BLK), :], own_ref.at[block], own_sems.at[block])

    def out_copy(n):
        return pltpu.make_async_copy(
            rows_ref.at[n], out_hbm.at[n * size:(n + 1) * size, :], out_sems.at[n])

    for n in range(count):
        front_copy(n).start()
        for j in range(GROUP):
            own_copy(n * GROUP + j).start()
    for n in range(count):
        front_copy(n).wait()
        for j in range(GROUP):
            block = n * GROUP + j
            own_copy(block).wait()
            rows = slice(j * BLK, (j + 1) * BLK)
            rows_ref[n, rows, :] += jnp.where(index[1, block] > 0, own_ref[block], 0.0)
        out_copy(n).start()
    for n in range(count):
        out_copy(n).wait()


def assemble(index, front, child):
    rows, cc = front.shape
    blocks = rows // BLK
    count = blocks // GROUP
    hbm = pl.BlockSpec(memory_space=pl.ANY)
    return pl.pallas_call(
        assemble_kernel,
        out_shape=jax.ShapeDtypeStruct((rows, cc), jnp.float32),
        in_specs=[pl.BlockSpec(memory_space=pltpu.SMEM), hbm, hbm],
        out_specs=hbm,
        scratch_shapes=[
            pltpu.VMEM((count, GROUP * BLK, cc), jnp.float32),
            pltpu.VMEM((blocks, BLK, cc), jnp.float32),
            pltpu.SemaphoreType.DMA((count,)),
            pltpu.SemaphoreType.DMA((blocks,)),
            pltpu.SemaphoreType.DMA((count,)),
        ],
        compiler_params=pltpu.CompilerParams(vmem_limit_bytes=52 * MIB),
        cost_estimate=pl.CostEstimate(
            flops=rows, bytes_accessed=16 * rows, transcendentals=0),
        name="assemble",
    )(index, front, child)


def finish_kernel(parts, place, index, base_hbm, recv_hbm, mult_ref, top_ref, *refs):
    pieces, refs = refs[:len(parts)], refs[len(parts):]
    out_hbm, rows_ref, piece_ref, recv_ref, base_sems, piece_sems, recv_sems, out_sems = refs
    cc = mult_ref.shape[1]
    is_pivot = place[0] < S // cc

    def start_of(n):
        slot, first, _ = parts[n]
        return pl.multiple_of(jnp.bitwise_xor(place[2], slot) * cc + first, parts[n][2])

    def held(ref, n):
        return ref.at[n, pl.ds(0, parts[n][2]), :]

    def rows_of(n):
        return pl.ds(start_of(n), parts[n][2])

    def base_copy(n):
        return pltpu.make_async_copy(base_hbm.at[rows_of(n), :], held(rows_ref, n), base_sems.at[n])

    def piece_copy(n):
        return pltpu.make_async_copy(pieces[n], held(piece_ref, n), piece_sems.at[n])

    def recv_copy(n, j, size):
        block = (start_of(n) + j) // BLK
        start = pl.multiple_of(index[2, block] * BLK + (parts[n][1] + j) % BLK, size)
        return pltpu.make_async_copy(
            recv_hbm.at[pl.ds(start, size), :], recv_ref.at[n, pl.ds(j, size), :],
            recv_sems.at[n, j // size])

    def out_copy(n):
        return pltpu.make_async_copy(held(rows_ref, n), out_hbm.at[rows_of(n), :], out_sems.at[n])

    def pieces_of(n):
        size = min(BLK, parts[n][2])
        return [(j, size) for j in range(0, parts[n][2], size)]

    for n in range(len(parts)):
        piece_copy(n).start()
        base_copy(n).start()
        for j, size in pieces_of(n):
            recv_copy(n, j, size).start()
    for n in range(len(parts)):
        piece_copy(n).wait()
        base_copy(n).wait()
        for j, size in pieces_of(n):
            recv_copy(n, j, size).wait()
        is_top = jnp.logical_and(place[1] == 0, start_of(n) < S)

        @pl.when(is_top)
        def _():
            held(rows_ref, n)[...] = top_ref[rows_of(n), :]

        @pl.when(jnp.logical_not(is_top))
        def _():
            product = lax.dot_general(
                held(piece_ref, n)[...], mult_ref[...], (((1,), (0,)), ((), ())),
                precision=lax.Precision.HIGH,
                preferred_element_type=jnp.float32,
            )
            for j, size in pieces_of(n):
                there = index[3, (start_of(n) + j) // BLK] > 0
                rows = pl.ds(j, size)
                base = rows_ref[n, rows, :] + jnp.where(there, recv_ref[n, rows, :], 0.0)
                rows_ref[n, rows, :] = jnp.where(is_pivot, 0.0, base) - product[j:j + size, :]

        out_copy(n).start()
    for n in range(len(parts)):
        out_copy(n).wait()


def finish(place, index, base, recv, parts, mult, top):
    rows, cc = base.shape
    count = len(parts)
    total = sum(piece.shape[0] for _, _, piece in parts)
    hbm = pl.BlockSpec(memory_space=pl.ANY)
    smem = pl.BlockSpec(memory_space=pltpu.SMEM)
    keys = tuple((slot, first, piece.shape[0]) for slot, first, piece in parts)
    return pl.pallas_call(
        functools.partial(finish_kernel, keys),
        out_shape=jax.ShapeDtypeStruct((rows, cc), jnp.float32),
        in_specs=[smem, smem, hbm, hbm] + vmem_specs(2) + [hbm] * count,
        out_specs=hbm,
        scratch_shapes=[
            pltpu.VMEM((count, cc, cc), jnp.float32),
            pltpu.VMEM((count, cc, S), jnp.float32),
            pltpu.VMEM((count, cc, cc), jnp.float32),
            pltpu.SemaphoreType.DMA((count,)),
            pltpu.SemaphoreType.DMA((count,)),
            pltpu.SemaphoreType.DMA((count, -(-cc // BLK))),
            pltpu.SemaphoreType.DMA((count,)),
        ],
        input_output_aliases={2: 0},
        compiler_params=pltpu.CompilerParams(vmem_limit_bytes=48 * MIB),
        cost_estimate=pl.CostEstimate(
            flops=6 * total * S * cc, bytes_accessed=4 * total * (3 * cc + S),
            transcendentals=0),
        name="finish",
    )(place, index, base, recv, mult, top, *[piece for _, _, piece in parts])


def block_places(blocks, first, count, shift, limit):
    parent = first + jnp.arange(count, dtype=jnp.int32)
    reached = jnp.sum((blocks[None, :] <= parent[:, None]).astype(jnp.int32), axis=1)
    there = jnp.sum((blocks[None, :] == parent[:, None]).astype(jnp.int32), axis=1)
    return jnp.clip(reached - 1 - shift, 0, limit - 1), there


def spread_pivot(cols, front_index, front_count, holders):
    leaf_index = lax.axis_index("leaf")
    half = S // 2
    mine = lax.dynamic_slice_in_dim(cols, leaf_index * half, half, 0)
    steps = []
    step = holders
    while step < front_count:
        steps.append(step)
        step *= 2
    pieces = []
    for order, part in ((steps, mine[:half // 2]), (steps[::-1], mine[half // 2:])):
        held = list(range(holders))
        part = jnp.where(front_index < holders, part, 0.0)
        for step in order:
            got = lax.ppermute(part, "front", [(f, f + step) for f in held])
            part = part + got
            held += [f + step for f in held]
        pieces.append(part)
    mine = jnp.concatenate(pieces, axis=0)
    if holders > 1:
        groups = [list(range(f, f + holders)) for f in range(0, front_count, holders)]
        mine = lax.all_gather(mine, "front", axis_index_groups=groups, axis=1, tiled=True)
    other = lax.ppermute(mine, "leaf", [(0, 1), (1, 0)])
    low = jnp.where(leaf_index == 0, mine, other)
    high = jnp.where(leaf_index == 0, other, mine)
    return jnp.concatenate([low, high], axis=0)


def pass_on(part, steps, n):
    held = [0]
    for step in steps[:n]:
        held += [f + step for f in held]
    return part + lax.ppermute(part, "front", [(f, f + steps[n]) for f in held])


def per_device(front_block, child_update, child_map):
    row_count, col_count = front_block.shape
    front_count = lax.axis_size("front")
    leaf_index = lax.axis_index("leaf")
    front_index = lax.axis_index("front")
    half = front_count // 2
    place = jnp.stack([front_index, leaf_index, front_index % half]).astype(jnp.int32)
    swap = [(0, 1), (1, 0)]
    child = child_update[0]
    blocks = child_map[0]
    child_blocks = blocks.shape[0]
    parent_blocks = row_count // BLK

    mine = pivot_rows(place, blocks, front_block, child)
    cols, piece, *packed = pivot_sum(place, mine, lax.ppermute(mine, "leaf", swap))

    pairs = [(f, f + half) for f in range(half)]
    pairs += [(front_count + f + half, front_count + f) for f in range(half)]
    came = lax.ppermute(piece, ("leaf", "front"), pairs)

    other_blocks = lax.ppermute(blocks, "leaf", swap)
    first = leaf_index * parent_blocks
    shift = leaf_index * (child_blocks - parent_blocks)
    index = jnp.stack(
        block_places(blocks, first, parent_blocks, 0, child_blocks)
        + block_places(other_blocks, first, parent_blocks, shift, parent_blocks))

    def across(value, bit):
        return lax.ppermute(value, "front", [(f, f ^ bit) for f in range(front_count)])

    barrier = lax.optimization_barrier
    own = (front_index >= half) == (leaf_index == 1)
    if packed:
        orders, step = [[1, 2], [2, 1]], 4
        while step <= half:
            for order in orders:
                order.append(step)
            step *= 2
        parts = [pass_on(part, order, 0) for part, order in zip(packed, orders)]
        parts, later = barrier((parts, leaf_index))
        sent = child_rows(later, child, row_count)
        parts = [pass_on(part, order, 1) for part, order in zip(parts, orders)]
        parts, sent, index = barrier((parts, sent, index))
        base = assemble(index, front_block, child)
        for n in range(2, len(orders[0]) - 1):
            parts = [pass_on(part, order, n) for part, order in zip(parts, orders)]
        parts, came, base = barrier((parts, came, base))
    else:
        sent = child_rows(leaf_index, child, row_count)
        base = assemble(index, front_block, child)
        sources = [spread_pivot(cols, front_index, front_count, S // col_count)]
    piece = jnp.where(own, piece, came)

    bit, slots, held = half // 2, [0], [piece]
    while bit > 4:
        held += [across(part, bit) for part in held]
        slots += [slot + bit for slot in slots]
        bit //= 2
    sides = [(across(part, 1), across(part, 2)) for part in held]
    if packed:
        parts = [pass_on(part, order, len(order) - 1) for part, order in zip(parts, orders)]
        parts, held = barrier((parts, held))
        sources = parts + [lax.ppermute(part, "leaf", swap) for part in parts]
    over = [across(part, 4) for part in held]
    sources, sides = barrier((sources, sides))
    cut = col_count // 2
    crossed = [(across(xs[:cut], 2), across(ys[cut:], 1)) for xs, ys in sides]
    u, x = first_step(place, sources)
    u, x = middle_step(1, u, x)
    u, x, over, crossed, sent = barrier((u, x, over, crossed, sent))
    recv = lax.ppermute(sent, "leaf", swap)
    over_sides = [(across(part, 1), across(part, 2)) for part in over]
    over_crossed = [(across(low, 4), across(high, 4)) for low, high in crossed]
    u, x = middle_step(2, u, x)
    top, mult = last_step(place, u, x, cols)

    early, late = [], []
    for group, first, alone, beside, cross in (
            (early, 0, held, sides, crossed), (late, 4, over, over_sides, over_crossed)):
        for slot, part, (xs, ys), (low, high) in zip(slots, alone, beside, cross):
            slot += first
            early.append((slot, 0, part))
            group += [(slot + 1, 0, xs), (slot + 2, 0, ys)]
            group += [(slot + 3, 0, low), (slot + 3, cut, high)]
    for group in (early, late):
        base = finish(place, index, base, recv, group, mult, top)
    return base


def solution(mesh):
    return jax.shard_map(
        per_device,
        mesh=mesh,
        in_specs=(P("leaf", "front"), P("leaf", None, "front"), P("leaf", None)),
        out_specs=P("leaf", "front"),
        check_vma=False,
    )
```

```python
import functools

import jax
import jax.numpy as jnp
from jax import lax
from jax.experimental import pallas as pl
from jax.experimental.pallas import tpu as pltpu
from jax.sharding import PartitionSpec as P

BLK = 128
S = 512
SUB = 8
MIB = 1024 * 1024


def lane_spread(tile, lane):
    return jnp.broadcast_to(tile[:, lane:lane + 1], tile.shape)


def row_spread(tile, row):
    return jnp.broadcast_to(tile[row:row + 1, :], tile.shape)


def eliminate_block(block):
    strips = BLK // SUB
    sub = lax.broadcasted_iota(jnp.int32, (SUB, BLK), 0)
    lane = lax.broadcasted_iota(jnp.int32, (SUB, BLK), 1)
    upper = [block[SUB * s:SUB * s + SUB, :] for s in range(strips)]
    lower = [jnp.where(lane == sub + SUB * s, 1.0, 0.0) for s in range(strips)]
    pivots = []
    for p in range(strips):
        first = SUB * p
        cols = [lane_spread(upper[p], first + j) for j in range(SUB)]
        a, x = upper[p], lower[p]
        recips = []
        pivot = jnp.zeros((SUB, BLK), jnp.float32)
        for j in range(SUB):
            d = row_spread(cols[j], j)
            recip = 1.0 / d
            recips.append(recip)
            pivot = jnp.where(sub == j, d, pivot)
            if j + 1 < SUB:
                m = jnp.where(sub > j, cols[j] * recip, 0.0)
                for k in range(j + 1, SUB):
                    cols[k] = cols[k] - m * row_spread(cols[k], j)
                a = a - m * row_spread(a, j)
                x = x - m * row_spread(x, j)
        upper[p], lower[p] = a, x
        pivots.append(pivot)
        if p + 1 == strips:
            break
        va = [row_spread(a, j) * recips[j] for j in range(SUB)]
        vx = [row_spread(x, j) * recips[j] for j in range(SUB)]
        for j in range(SUB - 2, -1, -1):
            for k in range(j + 1, SUB):
                c = row_spread(cols[k], j) * recips[j]
                va[j] = va[j] - c * va[k]
                vx[j] = vx[j] - c * vx[k]
        for s in range(p + 1, strips):
            b = [lane_spread(upper[s], first + j) for j in range(SUB)]
            upper[s] = upper[s] - (
                ((b[0] * va[0] + b[1] * va[1]) + (b[2] * va[2] + b[3] * va[3]))
                + ((b[4] * va[4] + b[5] * va[5]) + (b[6] * va[6] + b[7] * va[7]))
            )
            lower[s] = lower[s] - (
                ((b[0] * vx[0] + b[1] * vx[1]) + (b[2] * vx[2] + b[3] * vx[3]))
                + ((b[4] * vx[4] + b[5] * vx[5]) + (b[6] * vx[6] + b[7] * vx[7]))
            )
    return (
        jnp.concatenate(upper, axis=0),
        jnp.concatenate(lower, axis=0),
        jnp.concatenate(pivots, axis=0),
    )


def exact_dot(a, b, dims=((1,), (0,))):
    return lax.dot_general(
        a, b, (dims, ((), ())),
        precision=lax.Precision.HIGHEST,
        preferred_element_type=jnp.float32,
    )


def vmem_specs(count):
    return [pl.BlockSpec(memory_space=pltpu.VMEM)] * count


def pivot_rows_kernel(place, blocks, front_hbm, child_hbm, out_ref, front_ref, child_ref, sems):
    def copies(b):
        rows = slice(b * BLK, (b + 1) * BLK)
        return [
            pltpu.make_async_copy(hbm.at[rows, :], ref.at[rows, :], sems.at[n, b])
            for n, (hbm, ref) in enumerate(((front_hbm, front_ref), (child_hbm, child_ref)))]

    waits = [copies(b) for b in range(S // BLK)]
    for pair in waits:
        for copy in pair:
            copy.start()
    for b in range(S // BLK):
        for copy in waits[b]:
            copy.wait()
        rows = slice(b * BLK, (b + 1) * BLK)
        total = jnp.where(place[1] == 0, front_ref[rows, :], 0.0)
        for k in range(b + 1):
            total += jnp.where(blocks[k] == b, child_ref[k * BLK:(k + 1) * BLK, :], 0.0)
        out_ref[rows, :] = total


def pivot_rows(place, blocks, front, child):
    cc = front.shape[1]
    smem = pl.BlockSpec(memory_space=pltpu.SMEM)
    hbm = pl.BlockSpec(memory_space=pl.ANY)
    return pl.pallas_call(
        pivot_rows_kernel,
        out_shape=jax.ShapeDtypeStruct((S, cc), jnp.float32),
        in_specs=[smem, smem, hbm, hbm],
        out_specs=pl.BlockSpec(memory_space=pltpu.VMEM),
        scratch_shapes=[pltpu.VMEM((S, cc), jnp.float32)] * 2
        + [pltpu.SemaphoreType.DMA((2, S // BLK))],
        compiler_params=pltpu.CompilerParams(vmem_limit_bytes=54 * MIB),
        cost_estimate=pl.CostEstimate(
            flops=4 * S * cc, bytes_accessed=12 * S * cc, transcendentals=0),
        name="pivot_rows",
    )(place, blocks, front, child)


def child_rows_kernel(pieces, leaf, child_hbm, out_hbm, rows_ref, in_sems, out_sems):
    rows = out_hbm.shape[0]
    size = rows // pieces
    first = (1 - leaf[0]) * (child_hbm.shape[0] - rows)

    def in_copy(n):
        start = pl.multiple_of(first + n * size, BLK)
        return pltpu.make_async_copy(
            child_hbm.at[pl.ds(start, size), :], rows_ref.at[n], in_sems.at[n])

    def out_copy(n):
        return pltpu.make_async_copy(
            rows_ref.at[n], out_hbm.at[n * size:(n + 1) * size, :], out_sems.at[n])

    for n in range(pieces):
        in_copy(n).start()
    for n in range(pieces):
        in_copy(n).wait()
        out_copy(n).start()
    for n in range(pieces):
        out_copy(n).wait()


def child_rows(leaf, child, rows):
    pieces = 8
    hbm = pl.BlockSpec(memory_space=pl.ANY)
    return pl.pallas_call(
        functools.partial(child_rows_kernel, pieces),
        out_shape=jax.ShapeDtypeStruct((rows, child.shape[1]), jnp.float32),
        in_specs=[pl.BlockSpec(memory_space=pltpu.SMEM), hbm],
        out_specs=hbm,
        scratch_shapes=[pltpu.VMEM((pieces, rows // pieces, child.shape[1]), jnp.float32)]
        + [pltpu.SemaphoreType.DMA((pieces,))] * 2,
        compiler_params=pltpu.CompilerParams(vmem_limit_bytes=56 * MIB),
        cost_estimate=pl.CostEstimate(flops=0, bytes_accessed=4 * S, transcendentals=0),
        name="child_rows",
    )(leaf.reshape(1), child)


def packed_blocks():
    count = S // BLK
    order = [(i, j) for i in range(count) for j in range(i, count)]
    return order[:len(order) // 2], order[len(order) // 2:]


def block_slices(block):
    i, j = block
    return slice(i * BLK, (i + 1) * BLK), slice(j * BLK, (j + 1) * BLK)


def pivot_sum_kernel(place, mine_ref, other_ref, cols_ref, piece_ref, *packed):
    cols = mine_ref[...] + other_ref[...]
    cols_ref[...] = cols
    piece_ref[...] = cols.T
    if packed:
        size = packed[0].shape[0]
        for n, blocks in enumerate(zip(*packed_blocks())):
            low, high = (cols[block_slices(block)] for block in blocks)
            value = jnp.where(place[1] == 0, low, high)
            value = jnp.where(place[0] == 0, value, 0.0)
            for ref, start in zip(packed, (0, size)):
                begin = max(n * BLK, start)
                end = min((n + 1) * BLK, start + size)
                if begin < end:
                    ref[begin - start:end - start, :] = value[begin - n * BLK:end - n * BLK]


def pivot_sum(place, mine, other):
    cc = mine.shape[1]
    shapes = [(S, cc), (cc, S)]
    if cc == S:
        shapes += [(len(packed_blocks()[0]) * BLK // 2, BLK)] * 2
    return pl.pallas_call(
        pivot_sum_kernel,
        out_shape=[jax.ShapeDtypeStruct(shape, jnp.float32) for shape in shapes],
        in_specs=[pl.BlockSpec(memory_space=pltpu.SMEM)] + vmem_specs(2),
        out_specs=vmem_specs(len(shapes)),
        compiler_params=pltpu.CompilerParams(vmem_limit_bytes=16 * MIB),
        cost_estimate=pl.CostEstimate(
            flops=S * cc, bytes_accessed=16 * S * cc, transcendentals=0),
        name="pivot_sum",
    )(place, mine, other)


def factor_step(step, u_ref, x_ref):
    rows = slice(step * BLK, (step + 1) * BLK)
    done, rest = slice(0, (step + 1) * BLK), slice((step + 1) * BLK, S)
    block, inverse, pivots = eliminate_block(u_ref[rows, rows])
    scale = lax.rsqrt(pivots)
    scale = scale * (1.5 - 0.5 * pivots * scale * scale)
    r = lax.broadcasted_iota(jnp.int32, (BLK, BLK), 0)
    c = lax.broadcasted_iota(jnp.int32, (BLK, BLK), 1)
    u_ref[rows, rows] = jnp.where(c >= r, block * scale, 0.0)
    inverse = inverse * scale
    x = exact_dot(inverse, x_ref[rows, done])
    x_ref[rows, done] = x
    if step:
        u_ref[rows, :step * BLK] = jnp.zeros((BLK, step * BLK), jnp.float32)
    if step + 1 < S // BLK:
        u = exact_dot(inverse, u_ref[rows, rest])
        u_ref[rows, rest] = u
        u_ref[rest, rest] -= exact_dot(u, u, ((0,), (0,)))
        x_ref[rest, done] -= exact_dot(u, x, ((0,), (0,)))


def first_step_kernel(place, *refs):
    u_ref, x_ref = refs[-2:]
    sources = refs[:-2]
    if len(sources) == 1:
        u_ref[...] = sources[0][...]
    else:
        mine = jnp.concatenate([ref[...] for ref in sources[:2]], axis=0)
        other = jnp.concatenate([ref[...] for ref in sources[2:]], axis=0)
        values = [
            jnp.where(place[1] == 0, mine, other), jnp.where(place[1] == 0, other, mine)]
        for value, blocks in zip(values, packed_blocks()):
            for n, block in enumerate(blocks):
                u_ref[block_slices(block)] = value[n * BLK:(n + 1) * BLK]
    eye = lax.broadcasted_iota(jnp.int32, (S, S), 0) == lax.broadcasted_iota(
        jnp.int32, (S, S), 1)
    x_ref[...] = jnp.where(eye, 1.0, 0.0)
    factor_step(0, u_ref, x_ref)


def middle_step_kernel(step, u_in, x_in, u_ref, x_ref):
    u_ref[...] = u_in[...]
    x_ref[...] = x_in[...]
    factor_step(step, u_ref, x_ref)


FACTOR_PARAMS = dict(
    compiler_params=pltpu.CompilerParams(vmem_limit_bytes=48 * MIB),
    cost_estimate=pl.CostEstimate(
        flops=10 ** 6, bytes_accessed=4 * S, transcendentals=0),
)
SQUARE = jax.ShapeDtypeStruct((S, S), jnp.float32)


def first_step(place, sources):
    return pl.pallas_call(
        first_step_kernel,
        out_shape=[SQUARE] * 2,
        in_specs=[pl.BlockSpec(memory_space=pltpu.SMEM)] + vmem_specs(len(sources)),
        out_specs=vmem_specs(2),
        name="factor_step",
        **FACTOR_PARAMS,
    )(place, *sources)


def middle_step(step, u, x):
    return pl.pallas_call(
        functools.partial(middle_step_kernel, step),
        out_shape=[SQUARE] * 2,
        in_specs=vmem_specs(2),
        out_specs=vmem_specs(2),
        name="factor_step",
        **FACTOR_PARAMS,
    )(u, x)


def part_rows(place, part, cc):
    slot, first, size = part
    return pl.multiple_of(jnp.bitwise_xor(place[2], slot) * cc + first, size)


def fill_part(place, part, rows_ref, piece_ref, mult_ref, top_ref):
    cc = mult_ref.shape[1]
    start = part_rows(place, part, cc)
    is_top = jnp.logical_and(place[1] == 0, start < S)

    @pl.when(is_top)
    def _():
        rows_ref[...] = top_ref[pl.ds(start, part[2]), :]

    @pl.when(jnp.logical_not(is_top))
    def _():
        product = lax.dot_general(
            piece_ref[...], mult_ref[...], (((1,), (0,)), ((), ())),
            precision=lax.Precision.HIGH,
            preferred_element_type=jnp.float32,
        )
        rows_ref[...] = jnp.where(place[0] < S // cc, 0.0, rows_ref[...]) - product


def last_step_kernel(
        early, late, place, index, u_in, x_in, cols_ref, front_hbm, child_hbm, recv_hbm, *refs):
    pieces, refs = refs[:len(early)], refs[len(early):]
    out_hbm, top_ref, mult_ref, u_ref, x_ref, rows_ref, own_ref, recv_ref, piece_ref = refs[:9]
    rows_sems, own_sems, recv_sems, piece_sems, out_sems = refs[9:]
    cc = cols_ref.shape[1]
    parts = early + late

    def rows_of(n):
        return pl.ds(part_rows(place, parts[n], cc), parts[n][2])

    def held(ref, n):
        return ref.at[n, pl.ds(0, parts[n][2]), :]

    def subs(n):
        size = min(BLK, parts[n][2])
        return [(j, size) for j in range(0, parts[n][2], size)]

    def block_of(n, j):
        return (part_rows(place, parts[n], cc) + j) // BLK

    def child_copy(n, j, size, row, hbm, ref, sems):
        start = pl.multiple_of(
            index[row, block_of(n, j)] * BLK + (parts[n][1] + j) % BLK, size)
        return pltpu.make_async_copy(
            hbm.at[pl.ds(start, size), :], ref.at[n, pl.ds(j, size), :], sems.at[n, j // size])

    def loads(n):
        copies = [pltpu.make_async_copy(
            front_hbm.at[rows_of(n), :], held(rows_ref, n), rows_sems.at[n])]
        for j, size in subs(n):
            copies.append(child_copy(n, j, size, 0, child_hbm, own_ref, own_sems))
            copies.append(child_copy(n, j, size, 2, recv_hbm, recv_ref, recv_sems))
        if n < len(early):
            copies.append(
                pltpu.make_async_copy(pieces[n], held(piece_ref, n), piece_sems.at[n]))
        return copies

    started = [loads(n) for n in range(len(parts))]
    for copies in started:
        for copy in copies:
            copy.start()

    u_ref[...] = u_in[...]
    x_ref[...] = x_in[...]
    factor_step(S // BLK - 1, u_ref, x_ref)
    is_pivot = place[0] < S // cc
    start = pl.multiple_of(jnp.minimum(place[0], S // cc - 1) * cc, cc)
    solved = exact_dot(x_ref[...], cols_ref[...])
    top_ref[...] = jnp.where(is_pivot, u_ref[pl.ds(start, cc), :].T, solved)
    unit = lax.broadcasted_iota(jnp.int32, (S, cc), 0) == start + lax.broadcasted_iota(
        jnp.int32, (S, cc), 1)
    right = jnp.where(is_pivot, jnp.where(unit, -1.0, 0.0), solved)
    mult_ref[...] = exact_dot(x_ref[...], right, ((0,), (0,)))

    outs = []
    for n in list(range(len(early), len(parts))) + list(range(len(early))):
        for copy in started[n]:
            copy.wait()
        for j, size in subs(n):
            rows = pl.ds(j, size)
            block = block_of(n, j)
            total = rows_ref[n, rows, :]
            total += jnp.where(index[1, block] > 0, own_ref[n, rows, :], 0.0)
            total += jnp.where(index[3, block] > 0, recv_ref[n, rows, :], 0.0)
            rows_ref[n, rows, :] = total
        if n < len(early):
            fill_part(place, parts[n], held(rows_ref, n), held(piece_ref, n), mult_ref, top_ref)
        out = pltpu.make_async_copy(held(rows_ref, n), out_hbm.at[rows_of(n), :], out_sems.at[n])
        out.start()
        outs.append(out)
    for out in outs:
        out.wait()


def keys_of(parts):
    return tuple((slot, first, piece.shape[0]) for slot, first, piece in parts)


def last_step(place, index, u, x, cols, front, child, recv, early, late):
    rows, cc = front.shape
    count = len(early) + len(late)
    subs = -(-cc // BLK)
    hbm = pl.BlockSpec(memory_space=pl.ANY)
    smem = pl.BlockSpec(memory_space=pltpu.SMEM)
    dma = pltpu.SemaphoreType.DMA
    return pl.pallas_call(
        functools.partial(last_step_kernel, keys_of(early), late),
        out_shape=[jax.ShapeDtypeStruct((rows, cc), jnp.float32)]
        + [jax.ShapeDtypeStruct((S, cc), jnp.float32)] * 2,
        in_specs=[smem, smem] + vmem_specs(3) + [hbm] * (3 + len(early)),
        out_specs=[hbm] + vmem_specs(2),
        scratch_shapes=[pltpu.VMEM((S, S), jnp.float32)] * 2
        + [pltpu.VMEM((count, cc, cc), jnp.float32)] * 3
        + [pltpu.VMEM((len(early), cc, S), jnp.float32)]
        + [dma((count,)), dma((count, subs)), dma((count, subs)), dma((len(early),)),
           dma((count,))],
        compiler_params=pltpu.CompilerParams(vmem_limit_bytes=52 * MIB),
        cost_estimate=pl.CostEstimate(
            flops=10 ** 6, bytes_accessed=4 * S, transcendentals=0),
        name="factor_and_finish",
    )(place, index, u, x, cols, front, child, recv, *[piece for _, _, piece in early])


def finish_kernel(parts, place, base_hbm, mult_ref, top_ref, *refs):
    pieces, refs = refs[:len(parts)], refs[len(parts):]
    out_hbm, rows_ref, piece_ref, base_sems, piece_sems, out_sems = refs
    cc = mult_ref.shape[1]

    def rows_of(n):
        return pl.ds(part_rows(place, parts[n], cc), parts[n][2])

    def held(ref, n):
        return ref.at[n, pl.ds(0, parts[n][2]), :]

    loads = [
        (pltpu.make_async_copy(pieces[n], held(piece_ref, n), piece_sems.at[n]),
         pltpu.make_async_copy(base_hbm.at[rows_of(n), :], held(rows_ref, n), base_sems.at[n]))
        for n in range(len(parts))]
    for pair in loads:
        for copy in pair:
            copy.start()
    outs = []
    for n in range(len(parts)):
        for copy in loads[n]:
            copy.wait()
        fill_part(place, parts[n], held(rows_ref, n), held(piece_ref, n), mult_ref, top_ref)
        out = pltpu.make_async_copy(held(rows_ref, n), out_hbm.at[rows_of(n), :], out_sems.at[n])
        out.start()
        outs.append(out)
    for out in outs:
        out.wait()


def finish(place, base, parts, mult, top):
    rows, cc = base.shape
    count = len(parts)
    total = sum(piece.shape[0] for _, _, piece in parts)
    hbm = pl.BlockSpec(memory_space=pl.ANY)
    smem = pl.BlockSpec(memory_space=pltpu.SMEM)
    return pl.pallas_call(
        functools.partial(finish_kernel, keys_of(parts)),
        out_shape=jax.ShapeDtypeStruct((rows, cc), jnp.float32),
        in_specs=[smem, hbm] + vmem_specs(2) + [hbm] * count,
        out_specs=hbm,
        scratch_shapes=[
            pltpu.VMEM((count, cc, cc), jnp.float32),
            pltpu.VMEM((count, cc, S), jnp.float32),
        ]
        + [pltpu.SemaphoreType.DMA((count,))] * 3,
        input_output_aliases={1: 0},
        compiler_params=pltpu.CompilerParams(vmem_limit_bytes=48 * MIB),
        cost_estimate=pl.CostEstimate(
            flops=6 * total * S * cc, bytes_accessed=4 * total * (2 * cc + S),
            transcendentals=0),
        name="finish",
    )(place, base, mult, top, *[piece for _, _, piece in parts])


def block_places(blocks, first, count, shift, limit):
    parent = first + jnp.arange(count, dtype=jnp.int32)
    reached = jnp.sum((blocks[None, :] <= parent[:, None]).astype(jnp.int32), axis=1)
    there = jnp.sum((blocks[None, :] == parent[:, None]).astype(jnp.int32), axis=1)
    return jnp.clip(reached - 1 - shift, 0, limit - 1), there


def spread_pivot(cols, front_index, front_count, holders):
    leaf_index = lax.axis_index("leaf")
    half = S // 2
    mine = lax.dynamic_slice_in_dim(cols, leaf_index * half, half, 0)
    steps = []
    step = holders
    while step < front_count:
        steps.append(step)
        step *= 2
    pieces = []
    for order, part in ((steps, mine[:half // 2]), (steps[::-1], mine[half // 2:])):
        held = list(range(holders))
        part = jnp.where(front_index < holders, part, 0.0)
        for step in order:
            got = lax.ppermute(part, "front", [(f, f + step) for f in held])
            part = part + got
            held += [f + step for f in held]
        pieces.append(part)
    mine = jnp.concatenate(pieces, axis=0)
    if holders > 1:
        groups = [list(range(f, f + holders)) for f in range(0, front_count, holders)]
        mine = lax.all_gather(mine, "front", axis_index_groups=groups, axis=1, tiled=True)
    other = lax.ppermute(mine, "leaf", [(0, 1), (1, 0)])
    low = jnp.where(leaf_index == 0, mine, other)
    high = jnp.where(leaf_index == 0, other, mine)
    return jnp.concatenate([low, high], axis=0)


def pass_on(part, steps, n):
    held = [0]
    for step in steps[:n]:
        held += [f + step for f in held]
    return part + lax.ppermute(part, "front", [(f, f + steps[n]) for f in held])


def per_device(front_block, child_update, child_map):
    row_count, col_count = front_block.shape
    front_count = lax.axis_size("front")
    leaf_index = lax.axis_index("leaf")
    front_index = lax.axis_index("front")
    half = front_count // 2
    place = jnp.stack([front_index, leaf_index, front_index % half]).astype(jnp.int32)
    swap = [(0, 1), (1, 0)]
    child = child_update[0]
    blocks = child_map[0]
    child_blocks = blocks.shape[0]
    parent_blocks = row_count // BLK

    mine = pivot_rows(place, blocks, front_block, child)
    cols, piece, *packed = pivot_sum(place, mine, lax.ppermute(mine, "leaf", swap))

    pairs = [(f, f + half) for f in range(half)]
    pairs += [(front_count + f + half, front_count + f) for f in range(half)]
    came = lax.ppermute(piece, ("leaf", "front"), pairs)

    other_blocks = lax.ppermute(blocks, "leaf", swap)
    first = leaf_index * parent_blocks
    shift = leaf_index * (child_blocks - parent_blocks)
    index = jnp.stack(
        block_places(blocks, first, parent_blocks, 0, child_blocks)
        + block_places(other_blocks, first, parent_blocks, shift, parent_blocks))

    def across(value, bit):
        return lax.ppermute(value, "front", [(f, f ^ bit) for f in range(front_count)])

    barrier = lax.optimization_barrier
    own = (front_index >= half) == (leaf_index == 1)
    if packed:
        orders, step = [[1, 2], [2, 1]], 4
        while step <= half:
            for order in orders:
                order.append(step)
            step *= 2
        parts = [pass_on(part, order, 0) for part, order in zip(packed, orders)]
        parts, later = barrier((parts, leaf_index))
        sent = child_rows(later, child, row_count)
        parts = [pass_on(part, order, 1) for part, order in zip(parts, orders)]
        parts, sent, index = barrier((parts, sent, index))
        for n in range(2, len(orders[0]) - 1):
            parts = [pass_on(part, order, n) for part, order in zip(parts, orders)]
        parts, came, sent = barrier((parts, came, sent))
        recv = lax.ppermute(sent, "leaf", swap)
    else:
        recv = lax.ppermute(child_rows(leaf_index, child, row_count), "leaf", swap)
        sources = [spread_pivot(cols, front_index, front_count, S // col_count)]
    piece = jnp.where(own, piece, came)

    bit, slots, held = half // 2, [0], [piece]
    while bit > 4:
        held += [across(part, bit) for part in held]
        slots += [slot + bit for slot in slots]
        bit //= 2
    sides = [(across(part, 1), across(part, 2)) for part in held]
    if packed:
        parts = [pass_on(part, order, len(order) - 1) for part, order in zip(parts, orders)]
        parts, held = barrier((parts, held))
        sources = parts + [lax.ppermute(part, "leaf", swap) for part in parts]
    over = [across(part, 4) for part in held]
    cut = col_count // 2
    u, x = first_step(place, sources)
    u, x, sides = barrier((u, x, sides))
    crossed = [(across(xs[:cut], 2), across(ys[cut:], 1)) for xs, ys in sides]
    u, x = middle_step(1, u, x)
    u, x, over = barrier((u, x, over))
    over_sides = [(across(part, 1), across(part, 2)) for part in over]
    u, x = middle_step(2, u, x)
    u, x, crossed = barrier((u, x, crossed))
    over_crossed = [(across(low, 4), across(high, 4)) for low, high in crossed]

    early, late = [], []
    for group, first, alone, beside, cross in (
            (early, 0, held, sides, crossed), (late, 4, over, over_sides, over_crossed)):
        for slot, part, (xs, ys), (low, high) in zip(slots, alone, beside, cross):
            slot += first
            early.append((slot, 0, part))
            group += [(slot + 1, 0, xs), (slot + 2, 0, ys)]
            group += [(slot + 3, 0, low), (slot + 3, cut, high)]
    base, top, mult = last_step(
        place, index, u, x, cols, front_block, child, recv, early, keys_of(late))
    return finish(place, base, late, mult, top)


def solution(mesh):
    return jax.shard_map(
        per_device,
        mesh=mesh,
        in_specs=(P("leaf", "front"), P("leaf", None, "front"), P("leaf", None)),
        out_specs=P("leaf", "front"),
        check_vma=False,
    )
```

```python
import functools

import jax
import jax.numpy as jnp
from jax import lax
from jax.experimental import pallas as pl
from jax.experimental.pallas import tpu as pltpu
from jax.sharding import PartitionSpec as P

BLK = 128
S = 512
SUB = 8
MIB = 1024 * 1024


def lane_spread(tile, lane):
    return jnp.broadcast_to(tile[:, lane:lane + 1], tile.shape)


def row_spread(tile, row):
    return jnp.broadcast_to(tile[row:row + 1, :], tile.shape)


def eliminate_block(block):
    strips = BLK // SUB
    sub = lax.broadcasted_iota(jnp.int32, (SUB, BLK), 0)
    lane = lax.broadcasted_iota(jnp.int32, (SUB, BLK), 1)
    upper = [block[SUB * s:SUB * s + SUB, :] for s in range(strips)]
    lower = [jnp.where(lane == sub + SUB * s, 1.0, 0.0) for s in range(strips)]
    pivots = []
    for p in range(strips):
        first = SUB * p
        cols = [lane_spread(upper[p], first + j) for j in range(SUB)]
        a, x = upper[p], lower[p]
        recips = []
        pivot = jnp.zeros((SUB, BLK), jnp.float32)
        for j in range(SUB):
            d = row_spread(cols[j], j)
            recip = 1.0 / d
            recips.append(recip)
            pivot = jnp.where(sub == j, d, pivot)
            if j + 1 < SUB:
                m = jnp.where(sub > j, cols[j] * recip, 0.0)
                for k in range(j + 1, SUB):
                    cols[k] = cols[k] - m * row_spread(cols[k], j)
                a = a - m * row_spread(a, j)
                x = x - m * row_spread(x, j)
        upper[p], lower[p] = a, x
        pivots.append(pivot)
        if p + 1 == strips:
            break
        va = [row_spread(a, j) * recips[j] for j in range(SUB)]
        vx = [row_spread(x, j) * recips[j] for j in range(SUB)]
        for j in range(SUB - 2, -1, -1):
            for k in range(j + 1, SUB):
                c = row_spread(cols[k], j) * recips[j]
                va[j] = va[j] - c * va[k]
                vx[j] = vx[j] - c * vx[k]
        for s in range(p + 1, strips):
            b = [lane_spread(upper[s], first + j) for j in range(SUB)]
            upper[s] = upper[s] - (
                ((b[0] * va[0] + b[1] * va[1]) + (b[2] * va[2] + b[3] * va[3]))
                + ((b[4] * va[4] + b[5] * va[5]) + (b[6] * va[6] + b[7] * va[7]))
            )
            lower[s] = lower[s] - (
                ((b[0] * vx[0] + b[1] * vx[1]) + (b[2] * vx[2] + b[3] * vx[3]))
                + ((b[4] * vx[4] + b[5] * vx[5]) + (b[6] * vx[6] + b[7] * vx[7]))
            )
    return (
        jnp.concatenate(upper, axis=0),
        jnp.concatenate(lower, axis=0),
        jnp.concatenate(pivots, axis=0),
    )


def exact_dot(a, b, dims=((1,), (0,))):
    return lax.dot_general(
        a, b, (dims, ((), ())),
        precision=lax.Precision.HIGHEST,
        preferred_element_type=jnp.float32,
    )


def vmem_specs(count):
    return [pl.BlockSpec(memory_space=pltpu.VMEM)] * count


def pivot_rows_kernel(place, blocks, front_hbm, child_hbm, out_ref, front_ref, child_ref, sems):
    def copies(b):
        rows = slice(b * BLK, (b + 1) * BLK)
        return [
            pltpu.make_async_copy(hbm.at[rows, :], ref.at[rows, :], sems.at[n, b])
            for n, (hbm, ref) in enumerate(((front_hbm, front_ref), (child_hbm, child_ref)))]

    waits = [copies(b) for b in range(S // BLK)]
    for pair in waits:
        for copy in pair:
            copy.start()
    for b in range(S // BLK):
        for copy in waits[b]:
            copy.wait()
        rows = slice(b * BLK, (b + 1) * BLK)
        total = jnp.where(place[1] == 0, front_ref[rows, :], 0.0)
        for k in range(b + 1):
            total += jnp.where(blocks[k] == b, child_ref[k * BLK:(k + 1) * BLK, :], 0.0)
        out_ref[rows, :] = total


def pivot_rows(place, blocks, front, child):
    cc = front.shape[1]
    smem = pl.BlockSpec(memory_space=pltpu.SMEM)
    hbm = pl.BlockSpec(memory_space=pl.ANY)
    return pl.pallas_call(
        pivot_rows_kernel,
        out_shape=jax.ShapeDtypeStruct((S, cc), jnp.float32),
        in_specs=[smem, smem, hbm, hbm],
        out_specs=pl.BlockSpec(memory_space=pltpu.VMEM),
        scratch_shapes=[pltpu.VMEM((S, cc), jnp.float32)] * 2
        + [pltpu.SemaphoreType.DMA((2, S // BLK))],
        compiler_params=pltpu.CompilerParams(vmem_limit_bytes=54 * MIB),
        cost_estimate=pl.CostEstimate(
            flops=4 * S * cc, bytes_accessed=12 * S * cc, transcendentals=0),
        name="pivot_rows",
    )(place, blocks, front, child)


def packed_blocks():
    count = S // BLK
    order = [(i, j) for i in range(count) for j in range(i, count)]
    return order[:len(order) // 2], order[len(order) // 2:]


def block_slices(block):
    i, j = block
    return slice(i * BLK, (i + 1) * BLK), slice(j * BLK, (j + 1) * BLK)


def pivot_sum_kernel(place, mine_ref, other_ref, cols_ref, piece_ref, *packed):
    cols = mine_ref[...] + other_ref[...]
    cols_ref[...] = cols
    piece_ref[...] = cols.T
    if packed:
        size = packed[0].shape[0]
        for n, blocks in enumerate(zip(*packed_blocks())):
            low, high = (cols[block_slices(block)] for block in blocks)
            value = jnp.where(place[1] == 0, low, high)
            value = jnp.where(place[0] == 0, value, 0.0)
            for ref, start in zip(packed, (0, size)):
                begin = max(n * BLK, start)
                end = min((n + 1) * BLK, start + size)
                if begin < end:
                    ref[begin - start:end - start, :] = value[begin - n * BLK:end - n * BLK]


def pivot_sum(place, mine, other):
    cc = mine.shape[1]
    shapes = [(S, cc), (cc, S)]
    if cc == S:
        shapes += [(len(packed_blocks()[0]) * BLK // 2, BLK)] * 2
    return pl.pallas_call(
        pivot_sum_kernel,
        out_shape=[jax.ShapeDtypeStruct(shape, jnp.float32) for shape in shapes],
        in_specs=[pl.BlockSpec(memory_space=pltpu.SMEM)] + vmem_specs(2),
        out_specs=vmem_specs(len(shapes)),
        compiler_params=pltpu.CompilerParams(vmem_limit_bytes=16 * MIB),
        cost_estimate=pl.CostEstimate(
            flops=S * cc, bytes_accessed=16 * S * cc, transcendentals=0),
        name="pivot_sum",
    )(place, mine, other)


def factor_step(step, u_ref, x_ref, between=lambda: None):
    rows = slice(step * BLK, (step + 1) * BLK)
    done, rest = slice(0, (step + 1) * BLK), slice((step + 1) * BLK, S)
    block, inverse, pivots = eliminate_block(u_ref[rows, rows])
    between()
    scale = lax.rsqrt(pivots)
    scale = scale * (1.5 - 0.5 * pivots * scale * scale)
    r = lax.broadcasted_iota(jnp.int32, (BLK, BLK), 0)
    c = lax.broadcasted_iota(jnp.int32, (BLK, BLK), 1)
    u_ref[rows, rows] = jnp.where(c >= r, block * scale, 0.0)
    inverse = inverse * scale
    x = exact_dot(inverse, x_ref[rows, done])
    x_ref[rows, done] = x
    if step:
        u_ref[rows, :step * BLK] = jnp.zeros((BLK, step * BLK), jnp.float32)
    if step + 1 < S // BLK:
        u = exact_dot(inverse, u_ref[rows, rest])
        u_ref[rows, rest] = u
        u_ref[rest, rest] -= exact_dot(u, u, ((0,), (0,)))
        x_ref[rest, done] -= exact_dot(u, x, ((0,), (0,)))


def first_step_kernel(place, child_hbm, *refs):
    sources = refs[:-6]
    u_ref, x_ref, sent_hbm, rows_ref, in_sems, out_sems = refs[-6:]
    count, size = rows_ref.shape[:2]
    first = (1 - place[1]) * (child_hbm.shape[0] - count * size)
    ins = [
        pltpu.make_async_copy(
            child_hbm.at[pl.ds(pl.multiple_of(first + n * size, BLK), size), :],
            rows_ref.at[n], in_sems.at[n])
        for n in range(count)]
    outs = [
        pltpu.make_async_copy(
            rows_ref.at[n], sent_hbm.at[n * size:(n + 1) * size, :], out_sems.at[n])
        for n in range(count)]
    for copy in ins:
        copy.start()

    def between():
        for copy_in, copy_out in zip(ins, outs):
            copy_in.wait()
            copy_out.start()

    if len(sources) == 1:
        u_ref[...] = sources[0][...]
    else:
        mine = jnp.concatenate([ref[...] for ref in sources[:2]], axis=0)
        other = jnp.concatenate([ref[...] for ref in sources[2:]], axis=0)
        values = [
            jnp.where(place[1] == 0, mine, other), jnp.where(place[1] == 0, other, mine)]
        for value, blocks in zip(values, packed_blocks()):
            for n, block in enumerate(blocks):
                u_ref[block_slices(block)] = value[n * BLK:(n + 1) * BLK]
    eye = lax.broadcasted_iota(jnp.int32, (S, S), 0) == lax.broadcasted_iota(
        jnp.int32, (S, S), 1)
    x_ref[...] = jnp.where(eye, 1.0, 0.0)
    factor_step(0, u_ref, x_ref, between)
    for copy in outs:
        copy.wait()


def middle_step_kernel(step, u_in, x_in, u_ref, x_ref):
    u_ref[...] = u_in[...]
    x_ref[...] = x_in[...]
    factor_step(step, u_ref, x_ref)


FACTOR_PARAMS = dict(
    compiler_params=pltpu.CompilerParams(vmem_limit_bytes=48 * MIB),
    cost_estimate=pl.CostEstimate(
        flops=10 ** 6, bytes_accessed=4 * S, transcendentals=0),
)
SQUARE = jax.ShapeDtypeStruct((S, S), jnp.float32)


def first_step(place, sources, child, rows):
    pieces = 8
    cc = child.shape[1]
    hbm = pl.BlockSpec(memory_space=pl.ANY)
    return pl.pallas_call(
        first_step_kernel,
        out_shape=[SQUARE] * 2 + [jax.ShapeDtypeStruct((rows, cc), jnp.float32)],
        in_specs=[pl.BlockSpec(memory_space=pltpu.SMEM), hbm] + vmem_specs(len(sources)),
        out_specs=vmem_specs(2) + [hbm],
        scratch_shapes=[pltpu.VMEM((pieces, rows // pieces, cc), jnp.float32)]
        + [pltpu.SemaphoreType.DMA((pieces,))] * 2,
        name="factor_step",
        **FACTOR_PARAMS,
    )(place, child, *sources)


def middle_step(step, u, x):
    return pl.pallas_call(
        functools.partial(middle_step_kernel, step),
        out_shape=[SQUARE] * 2,
        in_specs=vmem_specs(2),
        out_specs=vmem_specs(2),
        name="factor_step",
        **FACTOR_PARAMS,
    )(u, x)


def part_rows(place, part, cc):
    slot, first, size = part
    return pl.multiple_of(jnp.bitwise_xor(place[2], slot) * cc + first, size)


def fill_part(place, part, rows_ref, piece_ref, mult_ref, top_ref):
    cc = mult_ref.shape[1]
    start = part_rows(place, part, cc)
    is_top = jnp.logical_and(place[1] == 0, start < S)

    @pl.when(is_top)
    def _():
        rows_ref[...] = top_ref[pl.ds(start, part[2]), :]

    @pl.when(jnp.logical_not(is_top))
    def _():
        product = lax.dot_general(
            piece_ref[...], mult_ref[...], (((1,), (0,)), ((), ())),
            precision=lax.Precision.HIGH,
            preferred_element_type=jnp.float32,
        )
        rows_ref[...] = jnp.where(place[0] < S // cc, 0.0, rows_ref[...]) - product


def last_step_kernel(
        early, late, place, index, u_in, x_in, cols_ref, front_hbm, child_hbm, recv_hbm, *refs):
    pieces, refs = refs[:len(early)], refs[len(early):]
    out_hbm, top_ref, mult_ref, u_ref, x_ref, rows_ref, own_ref, recv_ref, piece_ref = refs[:9]
    rows_sems, own_sems, recv_sems, piece_sems, out_sems = refs[9:]
    cc = cols_ref.shape[1]
    parts = early + late

    def rows_of(n):
        return pl.ds(part_rows(place, parts[n], cc), parts[n][2])

    def held(ref, n):
        return ref.at[n, pl.ds(0, parts[n][2]), :]

    def subs(n):
        size = min(BLK, parts[n][2])
        return [(j, size) for j in range(0, parts[n][2], size)]

    def block_of(n, j):
        return (part_rows(place, parts[n], cc) + j) // BLK

    def child_copy(n, j, size, row, hbm, ref, sems):
        start = pl.multiple_of(
            index[row, block_of(n, j)] * BLK + (parts[n][1] + j) % BLK, size)
        return pltpu.make_async_copy(
            hbm.at[pl.ds(start, size), :], ref.at[n, pl.ds(j, size), :], sems.at[n, j // size])

    def loads(n):
        copies = [pltpu.make_async_copy(
            front_hbm.at[rows_of(n), :], held(rows_ref, n), rows_sems.at[n])]
        for j, size in subs(n):
            copies.append(child_copy(n, j, size, 0, child_hbm, own_ref, own_sems))
            copies.append(child_copy(n, j, size, 2, recv_hbm, recv_ref, recv_sems))
        if n < len(early):
            copies.append(
                pltpu.make_async_copy(pieces[n], held(piece_ref, n), piece_sems.at[n]))
        return copies

    started = [loads(n) for n in range(len(parts))]
    for copies in started:
        for copy in copies:
            copy.start()

    u_ref[...] = u_in[...]
    x_ref[...] = x_in[...]
    factor_step(S // BLK - 1, u_ref, x_ref)
    is_pivot = place[0] < S // cc
    start = pl.multiple_of(jnp.minimum(place[0], S // cc - 1) * cc, cc)
    solved = exact_dot(x_ref[...], cols_ref[...])
    top_ref[...] = jnp.where(is_pivot, u_ref[pl.ds(start, cc), :].T, solved)
    unit = lax.broadcasted_iota(jnp.int32, (S, cc), 0) == start + lax.broadcasted_iota(
        jnp.int32, (S, cc), 1)
    right = jnp.where(is_pivot, jnp.where(unit, -1.0, 0.0), solved)
    mult_ref[...] = exact_dot(x_ref[...], right, ((0,), (0,)))

    outs = []
    for n in list(range(len(early), len(parts))) + list(range(len(early))):
        for copy in started[n]:
            copy.wait()
        for j, size in subs(n):
            rows = pl.ds(j, size)
            block = block_of(n, j)
            total = rows_ref[n, rows, :]
            total += jnp.where(index[1, block] > 0, own_ref[n, rows, :], 0.0)
            total += jnp.where(index[3, block] > 0, recv_ref[n, rows, :], 0.0)
            rows_ref[n, rows, :] = total
        if n < len(early):
            fill_part(place, parts[n], held(rows_ref, n), held(piece_ref, n), mult_ref, top_ref)
        out = pltpu.make_async_copy(held(rows_ref, n), out_hbm.at[rows_of(n), :], out_sems.at[n])
        out.start()
        outs.append(out)
    for out in outs:
        out.wait()


def keys_of(parts):
    return tuple((slot, first, piece.shape[0]) for slot, first, piece in parts)


def last_step(place, index, u, x, cols, front, child, recv, early, late):
    rows, cc = front.shape
    count = len(early) + len(late)
    subs = -(-cc // BLK)
    hbm = pl.BlockSpec(memory_space=pl.ANY)
    smem = pl.BlockSpec(memory_space=pltpu.SMEM)
    dma = pltpu.SemaphoreType.DMA
    return pl.pallas_call(
        functools.partial(last_step_kernel, keys_of(early), late),
        out_shape=[jax.ShapeDtypeStruct((rows, cc), jnp.float32)]
        + [jax.ShapeDtypeStruct((S, cc), jnp.float32)] * 2,
        in_specs=[smem, smem] + vmem_specs(3) + [hbm] * (3 + len(early)),
        out_specs=[hbm] + vmem_specs(2),
        scratch_shapes=[pltpu.VMEM((S, S), jnp.float32)] * 2
        + [pltpu.VMEM((count, cc, cc), jnp.float32)] * 3
        + [pltpu.VMEM((len(early), cc, S), jnp.float32)]
        + [dma((count,)), dma((count, subs)), dma((count, subs)), dma((len(early),)),
           dma((count,))],
        compiler_params=pltpu.CompilerParams(vmem_limit_bytes=48 * MIB),
        cost_estimate=pl.CostEstimate(
            flops=10 ** 6, bytes_accessed=4 * S, transcendentals=0),
        name="factor_and_finish",
    )(place, index, u, x, cols, front, child, recv, *[piece for _, _, piece in early])


def finish_kernel(parts, place, base_hbm, mult_ref, top_ref, *refs):
    pieces, refs = refs[:len(parts)], refs[len(parts):]
    out_hbm, rows_ref, piece_ref, base_sems, piece_sems, out_sems = refs
    cc = mult_ref.shape[1]

    def rows_of(n):
        return pl.ds(part_rows(place, parts[n], cc), parts[n][2])

    def held(ref, n):
        return ref.at[n, pl.ds(0, parts[n][2]), :]

    loads = [
        (pltpu.make_async_copy(pieces[n], held(piece_ref, n), piece_sems.at[n]),
         pltpu.make_async_copy(base_hbm.at[rows_of(n), :], held(rows_ref, n), base_sems.at[n]))
        for n in range(len(parts))]
    for pair in loads:
        for copy in pair:
            copy.start()
    outs = []
    for n in range(len(parts)):
        for copy in loads[n]:
            copy.wait()
        fill_part(place, parts[n], held(rows_ref, n), held(piece_ref, n), mult_ref, top_ref)
        out = pltpu.make_async_copy(held(rows_ref, n), out_hbm.at[rows_of(n), :], out_sems.at[n])
        out.start()
        outs.append(out)
    for out in outs:
        out.wait()


def finish(place, base, parts, mult, top):
    rows, cc = base.shape
    count = len(parts)
    total = sum(piece.shape[0] for _, _, piece in parts)
    hbm = pl.BlockSpec(memory_space=pl.ANY)
    smem = pl.BlockSpec(memory_space=pltpu.SMEM)
    return pl.pallas_call(
        functools.partial(finish_kernel, keys_of(parts)),
        out_shape=jax.ShapeDtypeStruct((rows, cc), jnp.float32),
        in_specs=[smem, hbm] + vmem_specs(2) + [hbm] * count,
        out_specs=hbm,
        scratch_shapes=[
            pltpu.VMEM((count, cc, cc), jnp.float32),
            pltpu.VMEM((count, cc, S), jnp.float32),
        ]
        + [pltpu.SemaphoreType.DMA((count,))] * 3,
        input_output_aliases={1: 0},
        compiler_params=pltpu.CompilerParams(vmem_limit_bytes=48 * MIB),
        cost_estimate=pl.CostEstimate(
            flops=6 * total * S * cc, bytes_accessed=4 * total * (2 * cc + S),
            transcendentals=0),
        name="finish",
    )(place, base, mult, top, *[piece for _, _, piece in parts])


def block_places(blocks, first, count, shift, limit):
    parent = first + jnp.arange(count, dtype=jnp.int32)
    reached = jnp.sum((blocks[None, :] <= parent[:, None]).astype(jnp.int32), axis=1)
    there = jnp.sum((blocks[None, :] == parent[:, None]).astype(jnp.int32), axis=1)
    return jnp.clip(reached - 1 - shift, 0, limit - 1), there


def spread_pivot(cols, front_index, front_count, holders):
    leaf_index = lax.axis_index("leaf")
    half = S // 2
    mine = lax.dynamic_slice_in_dim(cols, leaf_index * half, half, 0)
    steps = []
    step = holders
    while step < front_count:
        steps.append(step)
        step *= 2
    pieces = []
    for order, part in ((steps, mine[:half // 2]), (steps[::-1], mine[half // 2:])):
        held = list(range(holders))
        part = jnp.where(front_index < holders, part, 0.0)
        for step in order:
            got = lax.ppermute(part, "front", [(f, f + step) for f in held])
            part = part + got
            held += [f + step for f in held]
        pieces.append(part)
    mine = jnp.concatenate(pieces, axis=0)
    if holders > 1:
        groups = [list(range(f, f + holders)) for f in range(0, front_count, holders)]
        mine = lax.all_gather(mine, "front", axis_index_groups=groups, axis=1, tiled=True)
    other = lax.ppermute(mine, "leaf", [(0, 1), (1, 0)])
    low = jnp.where(leaf_index == 0, mine, other)
    high = jnp.where(leaf_index == 0, other, mine)
    return jnp.concatenate([low, high], axis=0)


def pass_on(part, steps, n):
    held = [0]
    for step in steps[:n]:
        held += [f + step for f in held]
    return part + lax.ppermute(part, "front", [(f, f + steps[n]) for f in held])


def per_device(front_block, child_update, child_map):
    row_count, col_count = front_block.shape
    front_count = lax.axis_size("front")
    leaf_index = lax.axis_index("leaf")
    front_index = lax.axis_index("front")
    half = front_count // 2
    place = jnp.stack([front_index, leaf_index, front_index % half]).astype(jnp.int32)
    swap = [(0, 1), (1, 0)]
    child = child_update[0]
    blocks = child_map[0]
    child_blocks = blocks.shape[0]
    parent_blocks = row_count // BLK

    mine = pivot_rows(place, blocks, front_block, child)
    cols, piece, *packed = pivot_sum(place, mine, lax.ppermute(mine, "leaf", swap))

    pairs = [(f, f + half) for f in range(half)]
    pairs += [(front_count + f + half, front_count + f) for f in range(half)]
    came = lax.ppermute(piece, ("leaf", "front"), pairs)

    other_blocks = lax.ppermute(blocks, "leaf", swap)
    first = leaf_index * parent_blocks
    shift = leaf_index * (child_blocks - parent_blocks)
    index = jnp.stack(
        block_places(blocks, first, parent_blocks, 0, child_blocks)
        + block_places(other_blocks, first, parent_blocks, shift, parent_blocks))

    def across(value, bit):
        return lax.ppermute(value, "front", [(f, f ^ bit) for f in range(front_count)])

    barrier = lax.optimization_barrier
    own = (front_index >= half) == (leaf_index == 1)
    if packed:
        orders, step = [[1, 2], [2, 1]], 4
        while step <= half:
            for order in orders:
                order.append(step)
            step *= 2
        parts = [pass_on(part, order, 0) for part, order in zip(packed, orders)]
        parts = barrier(parts)
        parts = [pass_on(part, order, 1) for part, order in zip(parts, orders)]
        parts, index = barrier((parts, index))
        for n in range(2, len(orders[0]) - 1):
            parts = [pass_on(part, order, n) for part, order in zip(parts, orders)]
        parts, came = barrier((parts, came))
    else:
        sources = [spread_pivot(cols, front_index, front_count, S // col_count)]
    piece = jnp.where(own, piece, came)

    bit, slots, held = half // 2, [0], [piece]
    while bit > 4:
        held += [across(part, bit) for part in held]
        slots += [slot + bit for slot in slots]
        bit //= 2
    sides = [(across(part, 1), across(part, 2)) for part in held]
    if packed:
        parts = [pass_on(part, order, len(order) - 1) for part, order in zip(parts, orders)]
        parts, held = barrier((parts, held))
        sources = parts + [lax.ppermute(part, "leaf", swap) for part in parts]
    over = [across(part, 4) for part in held]
    cut = col_count // 2
    u, x, sent = first_step(place, sources, child, row_count)
    u, x, sides = barrier((u, x, sides))
    crossed = [(across(xs[:cut], 2), across(ys[cut:], 1)) for xs, ys in sides]
    u, x = middle_step(1, u, x)
    u, x, over, crossed, sent = barrier((u, x, over, crossed, sent))
    recv = lax.ppermute(sent, "leaf", swap)
    over_sides = [(across(part, 1), across(part, 2)) for part in over]
    over_crossed = [(across(low, 4), across(high, 4)) for low, high in crossed]
    u, x = middle_step(2, u, x)

    early, late = [], []
    for group, first, alone, beside, cross in (
            (early, 0, held, sides, crossed), (late, 4, over, over_sides, over_crossed)):
        for slot, part, (xs, ys), (low, high) in zip(slots, alone, beside, cross):
            slot += first
            early.append((slot, 0, part))
            group += [(slot + 1, 0, xs), (slot + 2, 0, ys)]
            group += [(slot + 3, 0, low), (slot + 3, cut, high)]
    base, top, mult = last_step(
        place, index, u, x, cols, front_block, child, recv, early, keys_of(late))
    return finish(place, base, late, mult, top)


def solution(mesh):
    return jax.shard_map(
        per_device,
        mesh=mesh,
        in_specs=(P("leaf", "front"), P("leaf", None, "front"), P("leaf", None)),
        out_specs=P("leaf", "front"),
        check_vma=False,
    )
```

```python
import functools

import jax
import jax.numpy as jnp
from jax import lax
from jax.experimental import pallas as pl
from jax.experimental.pallas import tpu as pltpu
from jax.sharding import PartitionSpec as P

BLK = 128
S = 512
SUB = 8
MIB = 1024 * 1024


def lane_spread(tile, lane):
    return jnp.broadcast_to(tile[:, lane:lane + 1], tile.shape)


def row_spread(tile, row):
    return jnp.broadcast_to(tile[row:row + 1, :], tile.shape)


def eliminate_block(block):
    strips = BLK // SUB
    sub = lax.broadcasted_iota(jnp.int32, (SUB, BLK), 0)
    lane = lax.broadcasted_iota(jnp.int32, (SUB, BLK), 1)
    upper = [block[SUB * s:SUB * s + SUB, :] for s in range(strips)]
    lower = [jnp.where(lane == sub + SUB * s, 1.0, 0.0) for s in range(strips)]
    pivots = []
    for p in range(strips):
        first = SUB * p
        cols = [lane_spread(upper[p], first + j) for j in range(SUB)]
        a, x = upper[p], lower[p]
        recips = []
        pivot = jnp.zeros((SUB, BLK), jnp.float32)
        for j in range(SUB):
            d = row_spread(cols[j], j)
            recip = 1.0 / d
            recips.append(recip)
            pivot = jnp.where(sub == j, d, pivot)
            if j + 1 < SUB:
                m = jnp.where(sub > j, cols[j] * recip, 0.0)
                for k in range(j + 1, SUB):
                    cols[k] = cols[k] - m * row_spread(cols[k], j)
                a = a - m * row_spread(a, j)
                x = x - m * row_spread(x, j)
        upper[p], lower[p] = a, x
        pivots.append(pivot)
        if p + 1 == strips:
            break
        va = [row_spread(a, j) * recips[j] for j in range(SUB)]
        vx = [row_spread(x, j) * recips[j] for j in range(SUB)]
        for j in range(SUB - 2, -1, -1):
            for k in range(j + 1, SUB):
                c = row_spread(cols[k], j) * recips[j]
                va[j] = va[j] - c * va[k]
                vx[j] = vx[j] - c * vx[k]
        for s in range(p + 1, strips):
            b = [lane_spread(upper[s], first + j) for j in range(SUB)]
            upper[s] = upper[s] - (
                ((b[0] * va[0] + b[1] * va[1]) + (b[2] * va[2] + b[3] * va[3]))
                + ((b[4] * va[4] + b[5] * va[5]) + (b[6] * va[6] + b[7] * va[7]))
            )
            lower[s] = lower[s] - (
                ((b[0] * vx[0] + b[1] * vx[1]) + (b[2] * vx[2] + b[3] * vx[3]))
                + ((b[4] * vx[4] + b[5] * vx[5]) + (b[6] * vx[6] + b[7] * vx[7]))
            )
    return (
        jnp.concatenate(upper, axis=0),
        jnp.concatenate(lower, axis=0),
        jnp.concatenate(pivots, axis=0),
    )


def exact_dot(a, b, dims=((1,), (0,))):
    return lax.dot_general(
        a, b, (dims, ((), ())),
        precision=lax.Precision.HIGHEST,
        preferred_element_type=jnp.float32,
    )


def vmem_specs(count):
    return [pl.BlockSpec(memory_space=pltpu.VMEM)] * count


def pivot_rows_kernel(place, blocks, front_hbm, child_hbm, out_ref, front_ref, child_ref, sems):
    def copies(b):
        rows = slice(b * BLK, (b + 1) * BLK)
        return [
            pltpu.make_async_copy(hbm.at[rows, :], ref.at[rows, :], sems.at[n, b])
            for n, (hbm, ref) in enumerate(((front_hbm, front_ref), (child_hbm, child_ref)))]

    waits = [copies(b) for b in range(S // BLK)]
    for pair in waits:
        for copy in pair:
            copy.start()
    for b in range(S // BLK):
        for copy in waits[b]:
            copy.wait()
        rows = slice(b * BLK, (b + 1) * BLK)
        total = jnp.where(place[1] == 0, front_ref[rows, :], 0.0)
        for k in range(b + 1):
            total += jnp.where(blocks[k] == b, child_ref[k * BLK:(k + 1) * BLK, :], 0.0)
        out_ref[rows, :] = total


def pivot_rows(place, blocks, front, child):
    cc = front.shape[1]
    smem = pl.BlockSpec(memory_space=pltpu.SMEM)
    hbm = pl.BlockSpec(memory_space=pl.ANY)
    return pl.pallas_call(
        pivot_rows_kernel,
        out_shape=jax.ShapeDtypeStruct((S, cc), jnp.float32),
        in_specs=[smem, smem, hbm, hbm],
        out_specs=pl.BlockSpec(memory_space=pltpu.VMEM),
        scratch_shapes=[pltpu.VMEM((S, cc), jnp.float32)] * 2
        + [pltpu.SemaphoreType.DMA((2, S // BLK))],
        compiler_params=pltpu.CompilerParams(vmem_limit_bytes=54 * MIB),
        cost_estimate=pl.CostEstimate(
            flops=4 * S * cc, bytes_accessed=12 * S * cc, transcendentals=0),
        name="pivot_rows",
    )(place, blocks, front, child)


def packed_blocks():
    count = S // BLK
    order = [(i, j) for i in range(count) for j in range(i, count)]
    return order[:len(order) // 2], order[len(order) // 2:]


def block_slices(block):
    i, j = block
    return slice(i * BLK, (i + 1) * BLK), slice(j * BLK, (j + 1) * BLK)


def pivot_sum_kernel(place, mine_ref, other_ref, cols_ref, piece_ref, *packed):
    cols = mine_ref[...] + other_ref[...]
    cols_ref[...] = cols
    piece_ref[...] = cols.T
    if packed:
        size = packed[0].shape[0]
        for n, blocks in enumerate(zip(*packed_blocks())):
            low, high = (cols[block_slices(block)] for block in blocks)
            value = jnp.where(place[1] == 0, low, high)
            value = jnp.where(place[0] == 0, value, 0.0)
            for ref, start in zip(packed, (0, size)):
                begin = max(n * BLK, start)
                end = min((n + 1) * BLK, start + size)
                if begin < end:
                    ref[begin - start:end - start, :] = value[begin - n * BLK:end - n * BLK]


def pivot_sum(place, mine, other):
    cc = mine.shape[1]
    shapes = [(S, cc), (cc, S)]
    if cc == S:
        shapes += [(len(packed_blocks()[0]) * BLK // 2, BLK)] * 2
    return pl.pallas_call(
        pivot_sum_kernel,
        out_shape=[jax.ShapeDtypeStruct(shape, jnp.float32) for shape in shapes],
        in_specs=[pl.BlockSpec(memory_space=pltpu.SMEM)] + vmem_specs(2),
        out_specs=vmem_specs(len(shapes)),
        compiler_params=pltpu.CompilerParams(vmem_limit_bytes=16 * MIB),
        cost_estimate=pl.CostEstimate(
            flops=S * cc, bytes_accessed=16 * S * cc, transcendentals=0),
        name="pivot_sum",
    )(place, mine, other)


def factor_step(step, u_ref, x_ref, between=lambda: None):
    rows = slice(step * BLK, (step + 1) * BLK)
    done, rest = slice(0, (step + 1) * BLK), slice((step + 1) * BLK, S)
    between()
    block, inverse, pivots = eliminate_block(u_ref[rows, rows])
    scale = lax.rsqrt(pivots)
    scale = scale * (1.5 - 0.5 * pivots * scale * scale)
    r = lax.broadcasted_iota(jnp.int32, (BLK, BLK), 0)
    c = lax.broadcasted_iota(jnp.int32, (BLK, BLK), 1)
    u_ref[rows, rows] = jnp.where(c >= r, block * scale, 0.0)
    inverse = inverse * scale
    x = exact_dot(inverse, x_ref[rows, done])
    x_ref[rows, done] = x
    if step:
        u_ref[rows, :step * BLK] = jnp.zeros((BLK, step * BLK), jnp.float32)
    if step + 1 < S // BLK:
        u = exact_dot(inverse, u_ref[rows, rest])
        u_ref[rows, rest] = u
        u_ref[rest, rest] -= exact_dot(u, u, ((0,), (0,)))
        x_ref[rest, done] -= exact_dot(u, x, ((0,), (0,)))


def first_step_kernel(place, child_hbm, *refs):
    sources = refs[:-6]
    u_ref, x_ref, sent_hbm, rows_ref, in_sems, out_sems = refs[-6:]
    count, size = rows_ref.shape[:2]
    first = (1 - place[1]) * (child_hbm.shape[0] - count * size)
    ins = [
        pltpu.make_async_copy(
            child_hbm.at[pl.ds(pl.multiple_of(first + n * size, BLK), size), :],
            rows_ref.at[n], in_sems.at[n])
        for n in range(count)]
    outs = [
        pltpu.make_async_copy(
            rows_ref.at[n], sent_hbm.at[n * size:(n + 1) * size, :], out_sems.at[n])
        for n in range(count)]
    for copy in ins:
        copy.start()

    def between():
        for copy_in, copy_out in zip(ins, outs):
            copy_in.wait()
            copy_out.start()

    if len(sources) == 1:
        u_ref[...] = sources[0][...]
    else:
        mine = jnp.concatenate([ref[...] for ref in sources[:2]], axis=0)
        other = jnp.concatenate([ref[...] for ref in sources[2:]], axis=0)
        values = [
            jnp.where(place[1] == 0, mine, other), jnp.where(place[1] == 0, other, mine)]
        for value, blocks in zip(values, packed_blocks()):
            for n, block in enumerate(blocks):
                u_ref[block_slices(block)] = value[n * BLK:(n + 1) * BLK]
    eye = lax.broadcasted_iota(jnp.int32, (S, S), 0) == lax.broadcasted_iota(
        jnp.int32, (S, S), 1)
    x_ref[...] = jnp.where(eye, 1.0, 0.0)
    factor_step(0, u_ref, x_ref, between)
    for copy in outs:
        copy.wait()


def middle_step_kernel(step, u_in, x_in, u_ref, x_ref):
    u_ref[...] = u_in[...]
    x_ref[...] = x_in[...]
    factor_step(step, u_ref, x_ref)


FACTOR_PARAMS = dict(
    compiler_params=pltpu.CompilerParams(vmem_limit_bytes=48 * MIB),
    cost_estimate=pl.CostEstimate(
        flops=10 ** 6, bytes_accessed=4 * S, transcendentals=0),
)
SQUARE = jax.ShapeDtypeStruct((S, S), jnp.float32)


def first_step(place, sources, child, rows):
    pieces = 8
    cc = child.shape[1]
    hbm = pl.BlockSpec(memory_space=pl.ANY)
    return pl.pallas_call(
        first_step_kernel,
        out_shape=[SQUARE] * 2 + [jax.ShapeDtypeStruct((rows, cc), jnp.float32)],
        in_specs=[pl.BlockSpec(memory_space=pltpu.SMEM), hbm] + vmem_specs(len(sources)),
        out_specs=vmem_specs(2) + [hbm],
        scratch_shapes=[pltpu.VMEM((pieces, rows // pieces, cc), jnp.float32)]
        + [pltpu.SemaphoreType.DMA((pieces,))] * 2,
        name="factor_step",
        **FACTOR_PARAMS,
    )(place, child, *sources)


def middle_step(step, u, x):
    return pl.pallas_call(
        functools.partial(middle_step_kernel, step),
        out_shape=[SQUARE] * 2,
        in_specs=vmem_specs(2),
        out_specs=vmem_specs(2),
        name="factor_step",
        **FACTOR_PARAMS,
    )(u, x)


def part_rows(place, part, cc):
    slot, first, size = part
    return pl.multiple_of(jnp.bitwise_xor(place[2], slot) * cc + first, size)


def fill_part(place, part, rows_ref, piece_ref, mult_ref, top_ref):
    cc = mult_ref.shape[1]
    start = part_rows(place, part, cc)
    is_top = jnp.logical_and(place[1] == 0, start < S)

    @pl.when(is_top)
    def _():
        rows_ref[...] = top_ref[pl.ds(start, part[2]), :]

    @pl.when(jnp.logical_not(is_top))
    def _():
        product = lax.dot_general(
            piece_ref[...], mult_ref[...], (((1,), (0,)), ((), ())),
            precision=lax.Precision.HIGH,
            preferred_element_type=jnp.float32,
        )
        rows_ref[...] = jnp.where(place[0] < S // cc, 0.0, rows_ref[...]) - product


def last_step_kernel(
        early, late, place, index, u_in, x_in, cols_ref, front_hbm, child_hbm, recv_hbm, *refs):
    pieces, refs = refs[:len(early)], refs[len(early):]
    out_hbm, top_ref, mult_ref, u_ref, x_ref, rows_ref, own_ref, recv_ref, piece_ref = refs[:9]
    rows_sems, own_sems, recv_sems, piece_sems, out_sems = refs[9:]
    cc = cols_ref.shape[1]
    parts = early + late

    def rows_of(n):
        return pl.ds(part_rows(place, parts[n], cc), parts[n][2])

    def held(ref, n):
        return ref.at[n, pl.ds(0, parts[n][2]), :]

    def subs(n):
        size = min(BLK, parts[n][2])
        return [(j, size) for j in range(0, parts[n][2], size)]

    def block_of(n, j):
        return (part_rows(place, parts[n], cc) + j) // BLK

    def child_copy(n, j, size, row, hbm, ref, sems):
        start = pl.multiple_of(
            index[row, block_of(n, j)] * BLK + (parts[n][1] + j) % BLK, size)
        return pltpu.make_async_copy(
            hbm.at[pl.ds(start, size), :], ref.at[n, pl.ds(j, size), :], sems.at[n, j // size])

    def loads(n):
        copies = [pltpu.make_async_copy(
            front_hbm.at[rows_of(n), :], held(rows_ref, n), rows_sems.at[n])]
        for j, size in subs(n):
            copies.append(child_copy(n, j, size, 0, child_hbm, own_ref, own_sems))
            copies.append(child_copy(n, j, size, 2, recv_hbm, recv_ref, recv_sems))
        if n < len(early):
            copies.append(
                pltpu.make_async_copy(pieces[n], held(piece_ref, n), piece_sems.at[n]))
        return copies

    started = [loads(n) for n in range(len(parts))]
    for copies in started:
        for copy in copies:
            copy.start()

    u_ref[...] = u_in[...]
    x_ref[...] = x_in[...]
    factor_step(S // BLK - 1, u_ref, x_ref)
    is_pivot = place[0] < S // cc
    start = pl.multiple_of(jnp.minimum(place[0], S // cc - 1) * cc, cc)
    solved = exact_dot(x_ref[...], cols_ref[...])
    top_ref[...] = jnp.where(is_pivot, u_ref[pl.ds(start, cc), :].T, solved)
    unit = lax.broadcasted_iota(jnp.int32, (S, cc), 0) == start + lax.broadcasted_iota(
        jnp.int32, (S, cc), 1)
    right = jnp.where(is_pivot, jnp.where(unit, -1.0, 0.0), solved)
    mult_ref[...] = exact_dot(x_ref[...], right, ((0,), (0,)))

    outs = []
    for n in range(len(parts)):
        for copy in started[n]:
            copy.wait()
        for j, size in subs(n):
            rows = pl.ds(j, size)
            block = block_of(n, j)
            total = rows_ref[n, rows, :]
            total += jnp.where(index[1, block] > 0, own_ref[n, rows, :], 0.0)
            total += jnp.where(index[3, block] > 0, recv_ref[n, rows, :], 0.0)
            rows_ref[n, rows, :] = total
        if n < len(early):
            fill_part(place, parts[n], held(rows_ref, n), held(piece_ref, n), mult_ref, top_ref)
        out = pltpu.make_async_copy(held(rows_ref, n), out_hbm.at[rows_of(n), :], out_sems.at[n])
        out.start()
        outs.append(out)
    for out in outs:
        out.wait()


def keys_of(parts):
    return tuple((slot, first, piece.shape[0]) for slot, first, piece in parts)


def last_step(place, index, u, x, cols, front, child, recv, early, late):
    rows, cc = front.shape
    count = len(early) + len(late)
    subs = -(-cc // BLK)
    hbm = pl.BlockSpec(memory_space=pl.ANY)
    smem = pl.BlockSpec(memory_space=pltpu.SMEM)
    dma = pltpu.SemaphoreType.DMA
    return pl.pallas_call(
        functools.partial(last_step_kernel, keys_of(early), late),
        out_shape=[jax.ShapeDtypeStruct((rows, cc), jnp.float32)]
        + [jax.ShapeDtypeStruct((S, cc), jnp.float32)] * 2,
        in_specs=[smem, smem] + vmem_specs(3) + [hbm] * (3 + len(early)),
        out_specs=[hbm] + vmem_specs(2),
        scratch_shapes=[pltpu.VMEM((S, S), jnp.float32)] * 2
        + [pltpu.VMEM((count, cc, cc), jnp.float32)] * 3
        + [pltpu.VMEM((len(early), cc, S), jnp.float32)]
        + [dma((count,)), dma((count, subs)), dma((count, subs)), dma((len(early),)),
           dma((count,))],
        compiler_params=pltpu.CompilerParams(vmem_limit_bytes=48 * MIB),
        cost_estimate=pl.CostEstimate(
            flops=10 ** 6, bytes_accessed=4 * S, transcendentals=0),
        name="factor_and_finish",
    )(place, index, u, x, cols, front, child, recv, *[piece for _, _, piece in early])


def finish_kernel(parts, place, base_hbm, mult_ref, top_ref, *refs):
    pieces, refs = refs[:len(parts)], refs[len(parts):]
    out_hbm, rows_ref, piece_ref, base_sems, piece_sems, out_sems = refs
    cc = mult_ref.shape[1]

    def rows_of(n):
        return pl.ds(part_rows(place, parts[n], cc), parts[n][2])

    def held(ref, n):
        return ref.at[n, pl.ds(0, parts[n][2]), :]

    loads = [
        (pltpu.make_async_copy(pieces[n], held(piece_ref, n), piece_sems.at[n]),
         pltpu.make_async_copy(base_hbm.at[rows_of(n), :], held(rows_ref, n), base_sems.at[n]))
        for n in range(len(parts))]
    for pair in loads:
        for copy in pair:
            copy.start()
    outs = []
    for n in range(len(parts)):
        for copy in loads[n]:
            copy.wait()
        fill_part(place, parts[n], held(rows_ref, n), held(piece_ref, n), mult_ref, top_ref)
        out = pltpu.make_async_copy(held(rows_ref, n), out_hbm.at[rows_of(n), :], out_sems.at[n])
        out.start()
        outs.append(out)
    for out in outs:
        out.wait()


def finish(place, base, parts, mult, top):
    rows, cc = base.shape
    count = len(parts)
    total = sum(piece.shape[0] for _, _, piece in parts)
    hbm = pl.BlockSpec(memory_space=pl.ANY)
    smem = pl.BlockSpec(memory_space=pltpu.SMEM)
    return pl.pallas_call(
        functools.partial(finish_kernel, keys_of(parts)),
        out_shape=jax.ShapeDtypeStruct((rows, cc), jnp.float32),
        in_specs=[smem, hbm] + vmem_specs(2) + [hbm] * count,
        out_specs=hbm,
        scratch_shapes=[
            pltpu.VMEM((count, cc, cc), jnp.float32),
            pltpu.VMEM((count, cc, S), jnp.float32),
        ]
        + [pltpu.SemaphoreType.DMA((count,))] * 3,
        input_output_aliases={1: 0},
        compiler_params=pltpu.CompilerParams(vmem_limit_bytes=48 * MIB),
        cost_estimate=pl.CostEstimate(
            flops=6 * total * S * cc, bytes_accessed=4 * total * (2 * cc + S),
            transcendentals=0),
        name="finish",
    )(place, base, mult, top, *[piece for _, _, piece in parts])


def block_places(blocks, first, count, shift, limit):
    parent = first + jnp.arange(count, dtype=jnp.int32)
    reached = jnp.sum((blocks[None, :] <= parent[:, None]).astype(jnp.int32), axis=1)
    there = jnp.sum((blocks[None, :] == parent[:, None]).astype(jnp.int32), axis=1)
    return jnp.clip(reached - 1 - shift, 0, limit - 1), there


def spread_pivot(cols, front_index, front_count, holders):
    leaf_index = lax.axis_index("leaf")
    half = S // 2
    mine = lax.dynamic_slice_in_dim(cols, leaf_index * half, half, 0)
    steps = []
    step = holders
    while step < front_count:
        steps.append(step)
        step *= 2
    pieces = []
    for order, part in ((steps, mine[:half // 2]), (steps[::-1], mine[half // 2:])):
        held = list(range(holders))
        part = jnp.where(front_index < holders, part, 0.0)
        for step in order:
            got = lax.ppermute(part, "front", [(f, f + step) for f in held])
            part = part + got
            held += [f + step for f in held]
        pieces.append(part)
    mine = jnp.concatenate(pieces, axis=0)
    if holders > 1:
        groups = [list(range(f, f + holders)) for f in range(0, front_count, holders)]
        mine = lax.all_gather(mine, "front", axis_index_groups=groups, axis=1, tiled=True)
    other = lax.ppermute(mine, "leaf", [(0, 1), (1, 0)])
    low = jnp.where(leaf_index == 0, mine, other)
    high = jnp.where(leaf_index == 0, other, mine)
    return jnp.concatenate([low, high], axis=0)


def pass_on(part, steps, n):
    held = [0]
    for step in steps[:n]:
        held += [f + step for f in held]
    return part + lax.ppermute(part, "front", [(f, f + steps[n]) for f in held])


def per_device(front_block, child_update, child_map):
    row_count, col_count = front_block.shape
    front_count = lax.axis_size("front")
    leaf_index = lax.axis_index("leaf")
    front_index = lax.axis_index("front")
    half = front_count // 2
    place = jnp.stack([front_index, leaf_index, front_index % half]).astype(jnp.int32)
    swap = [(0, 1), (1, 0)]
    child = child_update[0]
    blocks = child_map[0]
    child_blocks = blocks.shape[0]
    parent_blocks = row_count // BLK

    mine = pivot_rows(place, blocks, front_block, child)
    cols, piece, *packed = pivot_sum(place, mine, lax.ppermute(mine, "leaf", swap))

    pairs = [(f, f + half) for f in range(half)]
    pairs += [(front_count + f + half, front_count + f) for f in range(half)]
    came = lax.ppermute(piece, ("leaf", "front"), pairs)

    other_blocks = lax.ppermute(blocks, "leaf", swap)
    first = leaf_index * parent_blocks
    shift = leaf_index * (child_blocks - parent_blocks)
    index = jnp.stack(
        block_places(blocks, first, parent_blocks, 0, child_blocks)
        + block_places(other_blocks, first, parent_blocks, shift, parent_blocks))

    def across(value, bit):
        return lax.ppermute(value, "front", [(f, f ^ bit) for f in range(front_count)])

    barrier = lax.optimization_barrier
    own = (front_index >= half) == (leaf_index == 1)
    if packed:
        orders, step = [[1, 2], [2, 1]], 4
        while step <= half:
            for order in orders:
                order.append(step)
            step *= 2
        parts = [pass_on(part, order, 0) for part, order in zip(packed, orders)]
        parts = barrier(parts)
        parts = [pass_on(part, order, 1) for part, order in zip(parts, orders)]
        parts, index = barrier((parts, index))
        for n in range(2, len(orders[0]) - 1):
            parts = [pass_on(part, order, n) for part, order in zip(parts, orders)]
        parts, came = barrier((parts, came))
    else:
        sources = [spread_pivot(cols, front_index, front_count, S // col_count)]
    piece = jnp.where(own, piece, came)

    bit, slots, held = half // 2, [0], [piece]
    while bit > 4:
        held += [across(part, bit) for part in held]
        slots += [slot + bit for slot in slots]
        bit //= 2
    sides = [(across(part, 1), across(part, 2)) for part in held]
    if packed:
        parts = [pass_on(part, order, len(order) - 1) for part, order in zip(parts, orders)]
        parts, held = barrier((parts, held))
        sources = parts + [lax.ppermute(part, "leaf", swap) for part in parts]
    over = [across(part, 4) for part in held]
    cut = col_count // 2
    u, x, sent = first_step(place, sources, child, row_count)
    u, x, sides = barrier((u, x, sides))
    crossed = [(across(xs[:cut], 2), across(ys[cut:], 1)) for xs, ys in sides]
    u, x = middle_step(1, u, x)
    u, x, over, crossed, sent = barrier((u, x, over, crossed, sent))
    recv = lax.ppermute(sent, "leaf", swap)
    over_sides = [(across(part, 1), across(part, 2)) for part in over]
    over_crossed = [(across(low, 4), across(high, 4)) for low, high in crossed]
    u, x = middle_step(2, u, x)

    early, late = [], []
    for group, first, alone, beside, cross in (
            (early, 0, held, sides, crossed), (late, 4, over, over_sides, over_crossed)):
        for slot, part, (xs, ys), (low, high) in zip(slots, alone, beside, cross):
            slot += first
            early.append((slot, 0, part))
            group += [(slot + 1, 0, xs), (slot + 2, 0, ys)]
            group += [(slot + 3, 0, low), (slot + 3, cut, high)]
    base, top, mult = last_step(
        place, index, u, x, cols, front_block, child, recv, early, keys_of(late))
    return finish(place, base, late, mult, top)


def solution(mesh):
    return jax.shard_map(
        per_device,
        mesh=mesh,
        in_specs=(P("leaf", "front"), P("leaf", None, "front"), P("leaf", None)),
        out_specs=P("leaf", "front"),
        check_vma=False,
    )
```
